256 devices in a mesh: tile: 8 (over y, x_hi), orient: 32 (over x_lo, z, core).
Axes of the slice: x: 4 (x_hi: 2, x_lo: 2; x = x_hi * 2 + x_lo), y: 4, z: 8, core: 2. Of those that a mesh axis runs over, the one named last changes fastest.
Arguments:
- micrograph_tiles: bfloat16 [16, 512, 512], P('tile'), as said below
- tile_offsets: int32 [16, 2], P('tile'), may hold values from 0 to 3584
- library: bfloat16 [64, 32, 128, 128], P('tile', 'orient'), as said below
- orient_ids: int32 [32, 2], P('orient'), may hold values from 0 to 63
Outputs:
- peak_score: float32 [16, 384, 384], P('tile')
- z_score: float32 [16, 384, 384], P('tile')
The draws below stay inside these ranges and needn't reach their ends.
Inputs may be any that keep to these rules, and one draw needn't show every extreme that they name: `micrograph_tiles`: real-valued pixel intensities of the tiles. `library`: real-valued projection densities.
All inputs are finite; a program needn't handle non-finite values.
Results may differ from the reference program's by a relative error of at most 0.0095.
Values may be sent and summed in bfloat16 or wider, within the bound.
No kernel may reach another device: no remote copies, remote signals or barrier semaphores. Data moves between devices by JAX's collectives and lax.ppermute only.
A program may use at most 64 MiB of HBM per device.

```python
import math
import jax
import jax.numpy as jnp
from jax import lax

PAD = 512
TPL = 128
VALID = 384
STEPS = 2
TILES = 16
LIB = 64
SHARDS = 32
SEARCH = 64


def draw_micrograph_tiles(key, part):
    subkeys = jax.random.split(key, 4)
    base_draw = jax.random.truncated_normal(subkeys[0], -6.0, 6.0, (TILES, PAD, PAD), jnp.float32)
    ramp_values = jnp.arange(TILES, dtype=jnp.float32) / max(TILES - 1, 1)
    tile_scale = jnp.exp(math.log(3.0) * ramp_values + jax.random.uniform(subkeys[1], (TILES,), jnp.float32, 0.0, math.log(4.0)))
    row_scale = jnp.exp(jax.random.uniform(subkeys[2], (TILES, PAD, 1), jnp.float32, 0.0, math.log(10.0)))
    col_scale = jnp.exp(jax.random.uniform(subkeys[3], (TILES, 1, PAD), jnp.float32, 0.0, math.log(10.0)))
    return (base_draw * tile_scale[:, None, None] * row_scale * col_scale).astype(jnp.bfloat16)


def draw_library(key, part):
    subkeys = jax.random.split(key, 3)
    base_draw = jax.random.truncated_normal(subkeys[0], -6.0, 6.0, (LIB, SHARDS, TPL, TPL), jnp.float32)
    row_scale = jnp.exp(jax.random.uniform(subkeys[1], (LIB, SHARDS, TPL, 1), jnp.float32, 0.0, math.log(10.0)))
    col_scale = jnp.exp(jax.random.uniform(subkeys[2], (LIB, SHARDS, 1, TPL), jnp.float32, 0.0, math.log(10.0)))
    return (base_draw * row_scale * col_scale).astype(jnp.bfloat16)


def with_ends(drawn, key, smallest, top_value):
    extent = drawn.shape
    place = [jax.random.randint(jax.random.fold_in(key, axis), (), 0, extent[axis]) for axis in range(len(extent))]
    drawn = drawn.at[tuple(place)].set(smallest)
    longest = extent.index(max(extent))
    place[longest] = (place[longest] + 1) % extent[longest]
    return drawn.at[tuple(place)].set(top_value)


def setup_inputs(seed: int = 0) -> dict:
    seeds = jax.random.split(jax.random.key(seed), 5)
    micrograph_tiles = draw_micrograph_tiles(jax.random.fold_in(seeds[4], 71), 0)
    tile_offsets = with_ends(jax.random.randint(seeds[1], (TILES, 2), 0, 3585), jax.random.fold_in(seeds[1], 1), 0, 3584).astype(jnp.int32)
    library = draw_library(jax.random.fold_in(seeds[4], 71), 0)
    orient_ids = with_ends(jax.random.randint(seeds[3], (SHARDS, STEPS), 0, LIB), jax.random.fold_in(seeds[3], 1), 0, LIB - 1).astype(jnp.int32)
    return {"micrograph_tiles": micrograph_tiles, "tile_offsets": tile_offsets, "library": library, "orient_ids": orient_ids}


AMPLITUDE = 0.07
DEFOCUS_BASE = 100.0
DEFOCUS_TILT = 0.002
FLOOR_SHARE = 0.25

def dft_tables(length):
    counter = jnp.arange(length, dtype=jnp.int32)
    product = counter[:, None] * counter[None, :] % length
    angle_table = product.astype(jnp.float32) * (2.0 * math.pi / length)
    return (jnp.cos(angle_table).astype(jnp.bfloat16), jnp.sin(angle_table).astype(jnp.bfloat16))

def frequency_squares(length):
    counter = jnp.arange(length, dtype=jnp.int32)
    signed = jnp.where(counter < length // 2, counter, counter - length)
    frequency = signed.astype(jnp.float32) / length
    return frequency[:, None] * frequency[:, None] + frequency[None, :] * frequency[None, :]

def batched(spec, left_op, right_op):
    return jnp.einsum(spec, left_op.astype(jnp.float32), right_op.astype(jnp.float32))

def forward_tiles(images, cosine_table, sine_table):
    half_real = batched('tij,jk->tik', images, cosine_table).astype(jnp.bfloat16)
    half_imag = (-batched('tij,jk->tik', images, sine_table)).astype(jnp.bfloat16)
    spec_real = batched('ij,tjk->tik', cosine_table, half_real) + batched('ij,tjk->tik', sine_table, half_imag)
    spec_imag = batched('ij,tjk->tik', cosine_table, half_imag) - batched('ij,tjk->tik', sine_table, half_real)
    return (spec_real, spec_imag)

def tile_filters(tile_offsets, whiten, length):
    squares_freq = frequency_squares(length)
    offsets = tile_offsets.astype(jnp.float32)
    defocus = DEFOCUS_BASE + DEFOCUS_TILT * (offsets[:, 0] - offsets[:, 1])
    phase_angle = math.pi * defocus[:, None, None] * squares_freq[None]
    contrast = -(math.sqrt(1.0 - AMPLITUDE * AMPLITUDE) * jnp.sin(phase_angle) + AMPLITUDE * jnp.cos(phase_angle))
    center = jnp.where(squares_freq > 0.0, 1.0, 0.0).astype(jnp.float32)
    return contrast * (whiten * center)[None]

def template_spectrum(template, cosine_table, sine_table):
    pattern_size = template.shape[0]
    tpl_real = jnp.dot(template, cosine_table[:pattern_size], preferred_element_type=jnp.float32).astype(jnp.bfloat16)
    tpl_imag = (-jnp.dot(template, sine_table[:pattern_size], preferred_element_type=jnp.float32)).astype(jnp.bfloat16)
    col_cos = cosine_table[:, :pattern_size]
    col_sin = sine_table[:, :pattern_size]
    base_real = jnp.dot(col_cos, tpl_real, preferred_element_type=jnp.float32) + jnp.dot(col_sin, tpl_imag, preferred_element_type=jnp.float32)
    base_imag = jnp.dot(col_cos, tpl_imag, preferred_element_type=jnp.float32) - jnp.dot(col_sin, tpl_real, preferred_element_type=jnp.float32)
    return (base_real, base_imag)

def correlate(base_real, base_imag, filters, white_real, white_imag, cosine_table, sine_table, valid_rows):
    length = cosine_table.shape[0]
    filt_real = base_real[None] * filters
    filt_imag = base_imag[None] * filters
    energy = lax.optimization_barrier(jnp.mean(filt_real * filt_real + filt_imag * filt_imag, axis=(1, 2), keepdims=True))
    norm_scale = lax.rsqrt(energy + 1e-06)
    norm_real = (filt_real * norm_scale).astype(jnp.bfloat16).astype(jnp.float32)
    norm_imag = (filt_imag * norm_scale).astype(jnp.bfloat16).astype(jnp.float32)
    wide_real = white_real.astype(jnp.float32)
    wide_imag = white_imag.astype(jnp.float32)
    prod_real = (wide_real * norm_real + wide_imag * norm_imag).astype(jnp.bfloat16)
    prod_imag = (wide_imag * norm_real - wide_real * norm_imag).astype(jnp.bfloat16)
    row_cos = cosine_table[:valid_rows]
    row_sin = sine_table[:valid_rows]
    mid_real = (batched('ij,tjk->tik', row_cos, prod_real) - batched('ij,tjk->tik', row_sin, prod_imag)).astype(jnp.bfloat16)
    mid_imag = (batched('ij,tjk->tik', row_cos, prod_imag) + batched('ij,tjk->tik', row_sin, prod_real)).astype(jnp.bfloat16)
    result = batched('tij,jk->tik', mid_real, cosine_table[:, :valid_rows]) - batched('tij,jk->tik', mid_imag, sine_table[:, :valid_rows])
    return result / length

def reference(micrograph_tiles, tile_offsets, library, orient_ids):
    cosine_table, sine_table = dft_tables(PAD)
    spec_real, spec_imag = forward_tiles(micrograph_tiles, cosine_table, sine_table)
    mean_power = lax.optimization_barrier(jnp.sum(spec_real * spec_real + spec_imag * spec_imag, axis=0)) / TILES
    whiten = lax.rsqrt(jnp.maximum(mean_power, FLOOR_SHARE * jnp.mean(mean_power)))
    white_real = (spec_real * whiten[None]).astype(jnp.bfloat16)
    white_imag = (spec_imag * whiten[None]).astype(jnp.bfloat16)
    filters = tile_filters(tile_offsets, whiten, PAD)
    shard_index = jnp.arange(SHARDS, dtype=jnp.int32)
    templates = library[orient_ids, shard_index[:, None]].reshape(SEARCH, TPL, TPL)

    def visit_template(state_tuple, template):
        running_peak, running_sum, squares = state_tuple
        base_real, base_imag = template_spectrum(template, cosine_table, sine_table)
        scores = correlate(base_real, base_imag, filters, white_real, white_imag, cosine_table, sine_table, VALID)
        return ((jnp.maximum(running_peak, scores), running_sum + scores, squares + scores * scores), None)
    initial = (jnp.full((TILES, VALID, VALID), -jnp.inf, jnp.float32), jnp.zeros((TILES, VALID, VALID), jnp.float32), jnp.zeros((TILES, VALID, VALID), jnp.float32))
    (running_peak, running_sum, squares), _ = lax.scan(visit_template, initial, templates)
    mean_score = running_sum / SEARCH
    variance = squares / SEARCH - mean_score * mean_score
    z_score = (running_peak - mean_score) * lax.rsqrt(variance + 1e-06)
    return (running_peak, z_score)
```

```python
import math

import jax
import jax.numpy as jnp
import ml_dtypes
import numpy as np
from jax import lax
from jax.experimental import pallas as pl
from jax.experimental.pallas import tpu as pltpu
from jax.sharding import PartitionSpec as P

LEN = 512
TPL = 128
VALID = 384
TILES = 16
SEARCH = 64
HALF = 272
PART = 96
PACK = 72
AMPLITUDE = 0.07
DEFOCUS_BASE = 100.0
DEFOCUS_TILT = 0.002
FLOOR_SHARE = 0.25
VMEM_LIMIT = 56 * 1024 * 1024

F32 = jnp.float32
BF16 = jnp.bfloat16


def tables():
    counter = np.arange(LEN)
    angle = 2.0 * np.pi * (counter[:, None] * counter[None, :] % LEN) / LEN
    cos = np.cos(angle).astype(ml_dtypes.bfloat16).astype(np.float32)
    sin = np.sin(angle).astype(ml_dtypes.bfloat16).astype(np.float32)
    cos_half, sin_half = np.zeros((2, HALF, LEN), np.float32)
    cos_half[: LEN // 2 + 1] = cos[: LEN // 2 + 1]
    sin_half[: LEN // 2 + 1] = sin[: LEN // 2 + 1]
    first = np.concatenate([cos, -sin], 1)
    second = np.block([[cos_half, sin_half], [-sin_half, cos_half]])
    tpl = TPL
    second_tpl = np.block(
        [[cos_half[:, :tpl], sin_half[:, :tpl]], [-sin_half[:, :tpl], cos_half[:, :tpl]]]
    )
    inner = np.zeros((4, 2 * LEN, 256), np.float32)
    for part in range(4):
        cols = slice(PART * part, PART * (part + 1))
        inner[part, :LEN, :PART] = cos[:, cols]
        inner[part, :LEN, 128 : 128 + PART] = sin[:, cols]
        inner[part, LEN:, :PART] = -sin[:, cols]
        inner[part, LEN:, 128 : 128 + PART] = cos[:, cols]
    middle = LEN // 2
    outer = np.concatenate([2.0 * cos[:VALID, :middle], -2.0 * sin[:VALID, :middle]], 1)
    outer[:, 0] = cos[:VALID, 0]
    outer[:, middle] = cos[:VALID, middle]
    return [np.asarray(a).astype(ml_dtypes.bfloat16) for a in (first, second, second_tpl, inner, outer)]


def dot(left, right):
    return jnp.dot(left, right, preferred_element_type=F32)


def forward_kernel(place, tile, first, second, spec, keep, send, stack):
    half = dot(tile[0], first[...])
    stack[:LEN] = half[:, :LEN].astype(BF16)
    stack[LEN:] = half[:, LEN:].astype(BF16)
    result = dot(second[...], stack[...])
    spec[...] = result
    real, imag = result[:HALF], result[HALF:]
    power = real * real + imag * imag
    left, right = power[:, :256], power[:, 256:]
    low = place[0] == 0
    keep[...] = jnp.where(low, left, right)
    send[...] = jnp.where(low, right, left).astype(BF16)


def search_kernel(
    place, spec, own, other, row_wave, col_wave, first, second_tpl, inner, outer,
    tpl0, tpl1, tpl2, tpl3, out0, out1, out2, out3,
    gain_r, gain_i, energy_w, pats, lines, prod, mid, peak, total, squares,
):
    low = place[0] == 0
    mine, theirs = own[...].astype(F32), other[...].astype(F32)
    left, right = jnp.where(low, mine, theirs), jnp.where(low, theirs, mine)
    power = jnp.concatenate([left, right], axis=1) * (1.0 / TILES)
    row = lax.broadcasted_iota(jnp.int32, (HALF, LEN), 0)
    col = lax.broadcasted_iota(jnp.int32, (HALF, LEN), 1)
    edge = (row == 0) | (row == LEN // 2)
    count = jnp.where(row > LEN // 2, 0.0, jnp.where(edge, 1.0, 2.0))
    mean = jnp.sum(power * count) * (1.0 / (LEN * LEN))
    inverse = 1.0 / jnp.maximum(power, FLOOR_SHARE * mean)
    wave = row_wave[:, 0:1] * col_wave[0:1, :] + row_wave[:, 1:2] * col_wave[1:2, :]
    wave = jnp.where(row + col > 0, -wave, 0.0)
    gain = wave * inverse
    gain_r[...] = spec[:HALF] * gain
    gain_i[...] = spec[HALF:] * gain
    energy_w[...] = wave * gain * count * (1.0 / (LEN * LEN))
    for index, tpl in enumerate((tpl0, tpl1, tpl2, tpl3)):
        pats[4 * TPL * index : 4 * TPL * (index + 1)] = tpl[...]
    peak[...] = jnp.full((VALID, 128), -jnp.inf, F32)
    total[...] = jnp.zeros((VALID, 128), F32)
    squares[...] = jnp.zeros((VALID, 128), F32)
    top_row = lax.broadcasted_iota(jnp.int32, (LEN // 2, 128), 0) == 0

    @pl.loop(0, 8)
    def _(pair):
        pattern = pats[pl.ds(pl.multiple_of(pair * 2 * TPL, 2 * TPL), 2 * TPL), :]
        half = dot(pattern, first[...]).astype(BF16)
        scales = []
        for which in range(2):
            rows = slice(TPL * which, TPL * (which + 1))
            lines[which, :TPL] = half[rows, :LEN]
            lines[which, TPL:] = half[rows, LEN:]
            base = dot(second_tpl[...], lines[which])
            base_r, base_i = base[:HALF], base[HALF:]
            energy = jnp.sum((base_r * base_r + base_i * base_i) * energy_w[...])
            scales.append(lax.rsqrt(jnp.full((1, 128), energy + 1e-06)) * (1.0 / LEN))
            prod[which, :, :LEN] = (gain_r[...] * base_r + gain_i[...] * base_i).astype(BF16)
            prod[which, :, LEN:] = (gain_i[...] * base_r - gain_r[...] * base_i).astype(BF16)
            part = dot(prod[which], inner[0])
            lanes = slice(128 * which, 128 * (which + 1))
            mid_r, mid_i = part[: LEN // 2, :128], part[: LEN // 2, 128:]
            nyquist = part[LEN // 2 : LEN // 2 + 1, :128]
            mid[: LEN // 2, lanes] = mid_r.astype(BF16)
            mid[LEN // 2 :, lanes] = jnp.where(top_row, nyquist, mid_i).astype(BF16)
        maps = dot(outer[...], mid[...])
        map0, map1 = maps[:, :128] * scales[0], maps[:, 128:] * scales[1]
        peak[...] = jnp.maximum(peak[...], jnp.maximum(map0, map1))
        total[...] += map0 + map1
        squares[...] += map0 * map0 + map1 * map1

    for index, out in enumerate((out0, out1, out2, out3)):
        start = pl.multiple_of(place[2 + index] * PART, PART)
        for slot, source in enumerate((peak, total, squares)):
            out[PART * slot : PART * (slot + 1)] = source[pl.ds(start, PART), :].astype(BF16)


def fold(block):
    lane = lax.broadcasted_iota(jnp.int32, (PACK, 128), 1)
    tail = block[PACK:PART]
    moved = [pltpu.roll(tail, 96 - 32 * i, 1) for i in range(3)]
    return jnp.where(lane < PART, block[:PACK], jnp.concatenate(moved, axis=0))


def unfold(block):
    lane = lax.broadcasted_iota(jnp.int32, (24, 128), 1)
    pieces = [pltpu.roll(block[24 * i : 24 * (i + 1)], (32 * i + 32) % 128, 1) for i in range(3)]
    tail = jnp.where(lane < 32, pieces[0], jnp.where(lane < 64, pieces[1], pieces[2]))
    return jnp.concatenate([block, tail], axis=0)


def score_kernel(own, got1, got2, got3, out):
    blocks = [ref[...].astype(F32) for ref in (own, got1, got2, got3)]
    peak = blocks[0][:PART]
    for block in blocks[1:]:
        peak = jnp.maximum(peak, block[:PART])
    sums = blocks[0][PART:] + blocks[1][PART:] + blocks[2][PART:] + blocks[3][PART:]
    mean = sums[:PART] * (1.0 / SEARCH)
    variance = sums[PART:] * (1.0 / SEARCH) - mean * mean
    score = (peak - mean) * lax.rsqrt(variance + 1e-06)
    out[...] = jnp.concatenate([fold(peak), fold(score)], axis=0).astype(BF16)


def spread_kernel(place, a0, a1, a2, a3, b0, b1, b2, b3, peak_out, score_out, held):
    for side, refs in enumerate(((a0, a1, a2, a3), (b0, b1, b2, b3))):
        for slot, ref in enumerate(refs):
            for index in range(4):
                held[side, slot, index] = ref[2 * PACK * index : 2 * PACK * (index + 1)].astype(F32)
    lane = lax.broadcasted_iota(jnp.int32, (PART, 128), 1)
    for side in range(2):
        tile = place[0] if side == 0 else 1 - place[0]
        for index in range(4):
            start = pl.multiple_of(place[2 + index] * PART, PART)
            pieces = [held[side, place[6 + target], index] for target in range(4)]
            for slot, out in enumerate((peak_out, score_out)):
                p0, p1, p2, p3 = [unfold(p[PACK * slot : PACK * (slot + 1)]) for p in pieces]
                one = jnp.where(lane < 96, p0, pltpu.roll(p1, 96, 1))
                two = jnp.where(lane < 64, pltpu.roll(p1, 96, 1), pltpu.roll(p2, 64, 1))
                three = jnp.where(lane < 32, pltpu.roll(p2, 64, 1), pltpu.roll(p3, 32, 1))
                for at, value in enumerate((one, two, three)):
                    out[tile, pl.ds(start, PART), 128 * at : 128 * (at + 1)] = value


def whole(*shape):
    return pl.BlockSpec(shape, lambda i, *_: (0,) * len(shape))


def call(kernel, outs, in_specs, out_specs, scratch, args, scalars=1, cost=None):
    return pl.pallas_call(
        kernel,
        out_shape=outs,
        grid_spec=pltpu.PrefetchScalarGridSpec(
            num_scalar_prefetch=scalars,
            grid=(1,),
            in_specs=in_specs,
            out_specs=out_specs,
            scratch_shapes=scratch,
        ),
        compiler_params=pltpu.CompilerParams(vmem_limit_bytes=VMEM_LIMIT),
        cost_estimate=cost,
    )(*args)


def shaped(dtype, *shape):
    return jax.ShapeDtypeStruct(shape, dtype)


def flip(value, axis, mask):
    size = lax.axis_size(axis)
    return lax.ppermute(value, axis, [(i, i ^ mask) for i in range(size)])


def body(micrograph_tiles, tile_offsets, library, orient_ids):
    first, second, second_tpl, inner, outer = [jnp.asarray(a) for a in tables()]
    slots = library.shape[0]
    tile_at, orient_at = lax.axis_index("tile"), lax.axis_index("orient")
    core = orient_at & 1
    column = (orient_at >> 4) * 2 + ((orient_at >> 1) & 1)
    group = (orient_at >> 2) & 3
    place = jnp.stack(
        [core, column]
        + [group ^ i for i in range(4)]
        + [column ^ i for i in range(4)]
    ).astype(jnp.int32)

    picked = []
    for step in range(2):
        chosen = orient_ids[0, step]
        slab = lax.dynamic_index_in_dim(library[:, 0], chosen % slots, 0, keepdims=False)
        picked.append(jnp.where(chosen // slots == tile_at, slab, 0).astype(BF16))
    pattern = jnp.concatenate(picked, axis=0)
    for mask in (2, 4, 1):
        pattern = pattern + flip(pattern, "tile", mask)
    pattern = jnp.concatenate([pattern, flip(pattern, "orient", 1)], axis=0)
    patterns = [pattern] + [flip(pattern, "orient", mask) for mask in (2, 16, 18)]

    spec, keep, send = call(
        forward_kernel,
        (shaped(F32, 2 * HALF, LEN), shaped(F32, HALF, 256), shaped(BF16, HALF, 256)),
        [
            pl.BlockSpec((1, LEN, LEN), lambda i, at: (at[0], 0, 0)),
            whole(LEN, 2 * LEN),
            whole(2 * HALF, 2 * LEN),
        ],
        (whole(2 * HALF, LEN), whole(HALF, 256), whole(HALF, 256)),
        [pltpu.VMEM((2 * LEN, LEN), BF16)],
        (place, micrograph_tiles, first, second),
    )
    power = keep + flip(send, "orient", 1).astype(F32)
    for mask in (2, 4, 1):
        power = power + flip(power.astype(BF16), "tile", mask).astype(F32)
    own = power.astype(BF16)
    other = flip(own, "orient", 1)

    offset = lax.dynamic_index_in_dim(tile_offsets, core, 0, keepdims=False).astype(F32)
    defocus = DEFOCUS_BASE + DEFOCUS_TILT * (offset[0] - offset[1])
    counter = jnp.arange(LEN, dtype=jnp.int32)
    frequency = jnp.where(counter < LEN // 2, counter, counter - LEN).astype(F32) / LEN
    phase = math.pi * defocus * (frequency * frequency)
    sine, cosine = jnp.sin(phase), jnp.cos(phase)
    strong = math.sqrt(1.0 - AMPLITUDE * AMPLITUDE)
    col_wave = jnp.stack([strong * cosine - AMPLITUDE * sine, strong * sine + AMPLITUDE * cosine])
    row_wave = jnp.stack([sine[:HALF], cosine[:HALF]], axis=1)

    parts = call(
        search_kernel,
        (shaped(BF16, 3 * PART, 128),) * 4,
        [
            whole(2 * HALF, LEN),
            whole(HALF, 256),
            whole(HALF, 256),
            whole(HALF, 2),
            whole(2, LEN),
            whole(TPL, 2 * LEN),
            whole(2 * HALF, 2 * TPL),
            pl.BlockSpec((1, 2 * LEN, 256), lambda i, at: (at[1], 0, 0)),
            whole(VALID, LEN),
        ]
        + [whole(4 * TPL, TPL)] * 4,
        (whole(3 * PART, 128),) * 4,
        [
            pltpu.VMEM((HALF, LEN), F32),
            pltpu.VMEM((HALF, LEN), F32),
            pltpu.VMEM((HALF, LEN), F32),
            pltpu.VMEM((16 * TPL, TPL), BF16),
            pltpu.VMEM((2, 2 * TPL, LEN), BF16),
            pltpu.VMEM((2, HALF, 2 * LEN), BF16),
            pltpu.VMEM((LEN, 256), BF16),
            pltpu.VMEM((VALID, 128), F32),
            pltpu.VMEM((VALID, 128), F32),
            pltpu.VMEM((VALID, 128), F32),
        ],
        (place, spec, own, other, row_wave, col_wave, first, second_tpl, inner, outer, *patterns),
    )
    got = [flip(parts[i], "orient", 4 * i) for i in range(1, 4)]
    scored = call(
        score_kernel,
        shaped(BF16, 2 * PACK, 128),
        [whole(3 * PART, 128)] * 4,
        whole(2 * PACK, 128),
        [],
        (parts[0], *got),
        scalars=0,
    )
    strip = jnp.concatenate([scored] + [flip(scored, "orient", 4 * i) for i in range(1, 4)], axis=0)
    strips = [strip] + [flip(strip, "orient", mask) for mask in (2, 16, 18)]
    twins = [flip(s, "orient", 1) for s in strips]
    return call(
        spread_kernel,
        (shaped(F32, 2, VALID, VALID),) * 2,
        [whole(8 * PACK, 128)] * 8,
        (whole(2, VALID, VALID),) * 2,
        [pltpu.VMEM((2, 4, 4, 2 * PACK, 128), F32)],
        (place, *strips, *twins),
    )


def solution(mesh):
    placed = (
        P("tile", None, None),
        P("tile", None),
        P("tile", "orient", None, None),
        P("orient", None),
    )
    return jax.shard_map(
        body,
        mesh=mesh,
        in_specs=placed,
        out_specs=(P("tile", None, None), P("tile", None, None)),
        check_vma=False,
    )
```

```python
import math

import jax
import jax.numpy as jnp
import ml_dtypes
import numpy as np
from jax import lax
from jax.experimental import pallas as pl
from jax.experimental.pallas import tpu as pltpu
from jax.sharding import PartitionSpec as P

LEN = 512
TPL = 128
VALID = 384
TILES = 16
SEARCH = 64
HALF = 272
SHARE = 80
PART = 96
PACK = 72
AMPLITUDE = 0.07
DEFOCUS_BASE = 100.0
DEFOCUS_TILT = 0.002
FLOOR_SHARE = 0.25

F32 = jnp.float32
BF16 = jnp.bfloat16


def tables():
    counter = np.arange(LEN)
    angle = 2.0 * np.pi * (counter[:, None] * counter[None, :] % LEN) / LEN
    cos = np.cos(angle).astype(ml_dtypes.bfloat16).astype(np.float32)
    sin = np.sin(angle).astype(ml_dtypes.bfloat16).astype(np.float32)
    both = np.concatenate([cos, sin], 1)
    first_tpl = np.concatenate([cos[:TPL], -sin[:TPL]], 1)
    cos_tpl, sin_tpl = cos[:HALF, :TPL], sin[:HALF, :TPL]
    second_tpl = np.block([[cos_tpl, sin_tpl], [-sin_tpl, cos_tpl]])
    inner = np.zeros((4, 2 * LEN, 256), np.float32)
    for part in range(4):
        cols = slice(PART * part, PART * (part + 1))
        inner[part, :LEN, :PART] = cos[:, cols]
        inner[part, :LEN, 128 : 128 + PART] = sin[:, cols]
        inner[part, LEN:, :PART] = -sin[:, cols]
        inner[part, LEN:, 128 : 128 + PART] = cos[:, cols]
    middle = LEN // 2
    outer = np.concatenate([2.0 * cos[:VALID, :middle], -2.0 * sin[:VALID, :middle]], 1)
    outer[:, 0] = cos[:VALID, 0]
    outer[:, middle] = cos[:VALID, middle]
    tables = (both, first_tpl, second_tpl, inner, outer)
    return [np.asarray(a).astype(ml_dtypes.bfloat16) for a in tables]


def dot(left, right):
    return jnp.dot(left, right, preferred_element_type=F32)


def at_core():
    return lax.axis_index("orient") & 1


def at_column():
    return (lax.axis_index("orient") >> 2) & 3


def at_group():
    orient = lax.axis_index("orient")
    return (orient >> 4) * 2 + ((orient >> 1) & 1)


def pick_kernel(ids, first, second, out):
    owner = lax.axis_index("tile")
    for step, slab in enumerate((first, second)):
        held = ids[0, step] // 8 == owner
        lanes = slice(TPL * step, TPL * (step + 1))
        out[:, lanes] = jnp.where(held, slab[0, 0].astype(F32), 0.0).astype(BF16)


def forward_kernel(tile, both, spec, keep, send, stack, power):
    half = dot(tile[0], both[...])
    real, imag = half[:, :LEN].astype(BF16), (-half[:, LEN:]).astype(BF16)
    stack[:LEN, :LEN], stack[LEN:, :LEN] = real, imag
    stack[:LEN, LEN:], stack[LEN:, LEN:] = imag, -real
    result = dot(both[:HALF, :], stack[...])
    spec[...] = result
    power[:HALF] = result[:, :LEN] * result[:, :LEN] + result[:, LEN:] * result[:, LEN:]
    power[HALF:] = jnp.zeros((4 * SHARE - HALF, LEN), F32)
    share = power[pl.ds(pl.multiple_of(at_group() * SHARE, SHARE), SHARE), :]
    left, right = share[:, :256], share[:, 256:]
    low = at_core() == 0
    keep[...] = jnp.where(low, left, right).astype(BF16)
    send[...] = jnp.where(low, right, left).astype(BF16)


def wave_kernel(offsets, out):
    core = at_core()
    shift = (offsets[core, 0] - offsets[core, 1]).astype(F32)
    defocus = DEFOCUS_BASE + DEFOCUS_TILT * shift
    row = lax.broadcasted_iota(jnp.int32, (HALF, 1), 0).astype(F32) * (1.0 / LEN)
    col = lax.broadcasted_iota(jnp.int32, (1, LEN), 1)
    col = jnp.where(col < LEN // 2, col, col - LEN).astype(F32) * (1.0 / LEN)
    row_phase, col_phase = math.pi * defocus * (row * row), math.pi * defocus * (col * col)
    sine, cosine = jnp.sin(col_phase), jnp.cos(col_phase)
    strong = math.sqrt(1.0 - AMPLITUDE * AMPLITUDE)
    by_sine, by_cosine = strong * cosine - AMPLITUDE * sine, strong * sine + AMPLITUDE * cosine
    wave = jnp.sin(row_phase) * by_sine + jnp.cos(row_phase) * by_cosine
    out[...] = jnp.where(row + jnp.abs(col) > 0.0, -wave, 0.0)


def fold(block):
    lane = lax.broadcasted_iota(jnp.int32, (PACK, 128), 1)
    tail = block[PACK:PART]
    moved = [pltpu.roll(tail, 96 - 32 * i, 1) for i in range(3)]
    return jnp.where(lane < PART, block[:PACK], jnp.concatenate(moved, axis=0))


def unfold(block):
    lane = lax.broadcasted_iota(jnp.int32, (24, 128), 1)
    pieces = [pltpu.roll(block[24 * i : 24 * (i + 1)], (32 * i + 32) % 128, 1) for i in range(3)]
    tail = jnp.where(lane < 32, pieces[0], jnp.where(lane < 64, pieces[1], pieces[2]))
    return jnp.concatenate([block, tail], axis=0)


def gains_of(spec, own, other, wave, gains, power):
    low, group = at_core() == 0, at_group()
    for share in range(4):
        start = pl.multiple_of((share ^ group) * SHARE, SHARE)
        mine, theirs = [ref[pl.ds(start, SHARE), :].astype(F32) for ref in (own, other)]
        rows = slice(SHARE * share, SHARE * (share + 1))
        power[rows, :256] = jnp.where(low, mine, theirs)
        power[rows, 256:] = jnp.where(low, theirs, mine)
    density = power[:HALF] * (1.0 / TILES)
    row = lax.broadcasted_iota(jnp.int32, (HALF, LEN), 0)
    edge = (row == 0) | (row == LEN // 2)
    count = jnp.where(row > LEN // 2, 0.0, jnp.where(edge, 1.0, 2.0))
    mean = jnp.sum(density * count) * (1.0 / (LEN * LEN))
    gain = wave[...] / jnp.maximum(density, FLOOR_SHARE * mean)
    gains[0] = spec[:, :LEN] * gain
    gains[1] = spec[:, LEN:] * gain
    gains[2] = wave[...] * gain * count * (1.0 / (LEN * LEN))


def search(pats, gains, first, second_tpl, inner, outer, lines, prod, mid, before, sums):
    top_row = lax.broadcasted_iota(jnp.int32, (LEN // 2, 128), 0) == 0
    scales = []
    for rows in range(4):
        pattern = pats[TPL * rows : TPL * (rows + 1), :]
        for side in range(2):
            which = 2 * rows + side
            half = dot(pattern[:, TPL * side : TPL * (side + 1)], first[...]).astype(BF16)
            lines[which, :TPL] = half[:, :LEN]
            lines[which, TPL:] = half[:, LEN:]
    for which in range(8):
        base = dot(second_tpl[...], lines[which])
        base_r, base_i = base[:HALF], base[HALF:]
        energy = jnp.sum((base_r * base_r + base_i * base_i) * gains[2])
        scales.append(lax.rsqrt(jnp.full((1, 128), energy + 1e-06)) * (1.0 / LEN))
        prod[which, :, :LEN] = (gains[0] * base_r + gains[1] * base_i).astype(BF16)
        prod[which, :, LEN:] = (gains[1] * base_r - gains[0] * base_i).astype(BF16)
        part = dot(prod[which], inner[...])
        pair, lanes = which // 2, slice(128 * (which % 2), 128 * (which % 2 + 1))
        mid_r, mid_i = part[: LEN // 2, :128], part[: LEN // 2, 128:]
        nyquist = part[LEN // 2 : LEN // 2 + 1, :128]
        mid[pair, : LEN // 2, lanes] = mid_r.astype(BF16)
        mid[pair, LEN // 2 :, lanes] = jnp.where(top_row, nyquist, mid_i).astype(BF16)
        if which % 2 == 0:
            continue
        maps = dot(outer[...], mid[pair])
        map0, map1 = maps[:, :128] * scales[-2], maps[:, 128:] * scales[-1]
        most, both, power2 = jnp.maximum(map0, map1), map0 + map1, map0 * map0 + map1 * map1
        if before is not None:
            most = jnp.maximum(before[0], most)
            both, power2 = before[1] + both, before[2] + power2
        sums[0], sums[1], sums[2] = most, both, power2
        before = sums


def search_kernel(
    spec, own, other, wave, pats, first, second_tpl, inner, outer, gains, sums,
    power, lines, prod, mid,
):
    gains_of(spec, own, other, wave, gains, power)
    search(pats, gains, first, second_tpl, inner, outer, lines, prod, mid, None, sums)


def second_search_kernel(
    gains, before, pats, first, second_tpl, inner, outer, out0, out1, out2, out3,
    lines, prod, mid, sums,
):
    search(pats, gains, first, second_tpl, inner, outer, lines, prod, mid, before, sums)
    group = at_group()
    for index, out in enumerate((out0, out1, out2, out3)):
        rows = pl.ds(pl.multiple_of((group ^ index) * PART, PART), PART)
        folded = [fold(sums[slot, rows, :]) for slot in range(3)]
        folded.append(jnp.zeros((8, 128), F32))
        out[...] = jnp.concatenate(folded, axis=0).astype(BF16)


def score_kernel(own, got1, got2, got3, out):
    blocks = [ref[...].astype(F32) for ref in (own, got1, got2, got3)]
    peak = blocks[0][:PACK]
    for block in blocks[1:]:
        peak = jnp.maximum(peak, block[:PACK])
    total, squares = [
        sum(block[PACK * i : PACK * (i + 1)] for block in blocks) * (1.0 / SEARCH) for i in (1, 2)
    ]
    variance = squares - total * total
    score = (peak - total) * lax.rsqrt(variance + 1e-06)
    block = jnp.concatenate([peak, score], axis=0).astype(BF16)
    out[...] = block


def spread_kernel(place, *refs):
    peak_out, score_out = refs[8:]
    lane = lax.broadcasted_iota(jnp.int32, (PART, 128), 1)
    column, group = at_column(), at_group()

    def spread(strips):
        for number, strip in enumerate(strips):
            pieces = []
            for target in range(4):
                start = pl.multiple_of((column ^ target) * (2 * PACK), 2 * PACK)
                pieces.append(strip[pl.ds(start, 2 * PACK), :].astype(F32))
            rows = pl.ds(pl.multiple_of((group ^ number) * PART, PART), PART)
            for slot, out in enumerate((peak_out, score_out)):
                p0, p1, p2, p3 = [unfold(p[PACK * slot : PACK * (slot + 1)]) for p in pieces]
                p1, p2, p3 = [pltpu.roll(p, by, 1) for p, by in ((p1, 96), (p2, 64), (p3, 32))]
                out[0, rows, :128] = jnp.where(lane < 96, p0, p1)
                out[0, rows, 128:256] = jnp.where(lane < 64, p1, p2)
                out[0, rows, 256:] = jnp.where(lane < 32, p2, p3)

    pl.when(pl.program_id(0) == 0)(lambda: spread(refs[:4]))
    pl.when(pl.program_id(0) == 1)(lambda: spread(refs[4:8]))


VMEM = pl.BlockSpec(memory_space=pltpu.VMEM)
SMEM = pl.BlockSpec(memory_space=pltpu.SMEM)


def shaped(dtype, *shape):
    return jax.ShapeDtypeStruct(shape, dtype)


def limits(megabytes):
    return pltpu.CompilerParams(vmem_limit_bytes=megabytes * 1024 * 1024)


def cost(mega_products, megabytes):
    return pl.CostEstimate(
        flops=2_000_000 * mega_products, bytes_accessed=1_000_000 * megabytes, transcendentals=0
    )


def flip(value, axis, mask):
    size = lax.axis_size(axis)
    return lax.ppermute(value, axis, [(i, i ^ mask) for i in range(size)])


def body(micrograph_tiles, tile_offsets, library, orient_ids):
    both, first_tpl, second_tpl, inner, outer = [jnp.asarray(a) for a in tables()]

    pattern = pl.pallas_call(
        pick_kernel,
        out_shape=shaped(BF16, TPL, 2 * TPL),
        grid_spec=pltpu.PrefetchScalarGridSpec(
            num_scalar_prefetch=1,
            grid=(1,),
            in_specs=[
                pl.BlockSpec((1, 1, TPL, TPL), lambda i, ids: (ids[0, 0] % 8, 0, 0, 0)),
                pl.BlockSpec((1, 1, TPL, TPL), lambda i, ids: (ids[0, 1] % 8, 0, 0, 0)),
            ],
            out_specs=pl.BlockSpec((TPL, 2 * TPL), lambda i, ids: (0, 0)),
        ),
    )(orient_ids, library, library)
    micrograph_tiles, pattern = lax.optimization_barrier((micrograph_tiles, pattern))
    passed = flip(pattern, "tile", 1)

    spec, power, send = pl.pallas_call(
        forward_kernel,
        out_shape=(shaped(F32, HALF, 2 * LEN), shaped(BF16, SHARE, 256), shaped(BF16, SHARE, 256)),
        grid=(1,),
        in_specs=[
            pl.BlockSpec((1, LEN, LEN), lambda i: (at_core(), 0, 0)),
            pl.BlockSpec((LEN, 2 * LEN), lambda i: (0, 0)),
        ],
        out_specs=(
            pl.BlockSpec((HALF, 2 * LEN), lambda i: (0, 0)),
            pl.BlockSpec((SHARE, 256), lambda i: (0, 0)),
            pl.BlockSpec((SHARE, 256), lambda i: (0, 0)),
        ),
        scratch_shapes=[pltpu.VMEM((2 * LEN, 2 * LEN), BF16), pltpu.VMEM((4 * SHARE, LEN), F32)],
        compiler_params=limits(56),
        cost_estimate=cost(545, 3),
    )(micrograph_tiles, both)
    def add(left, right):
        return (left.astype(F32) + right.astype(F32)).astype(BF16)

    send, passed = lax.optimization_barrier((send, passed))
    message = jnp.concatenate([add(power, flip(send, "orient", 1)), add(pattern, passed)], axis=0)
    message, tile_offsets = lax.optimization_barrier((message, tile_offsets))
    message_2 = flip(message, "tile", 2)
    wave = pl.pallas_call(
        wave_kernel,
        out_shape=shaped(F32, HALF, LEN),
        in_specs=[SMEM],
        out_specs=VMEM,
        cost_estimate=cost(400, 1),
    )(tile_offsets)

    message = add(message, message_2)
    message, wave, inner = lax.optimization_barrier((message, wave, inner))
    message_6 = flip(message, "tile", 6)
    inner = lax.dynamic_index_in_dim(inner, at_column(), 0, keepdims=False)
    message = add(message, message_6)
    message, inner = lax.optimization_barrier((message, inner))
    power, pattern = message[:SHARE], message[SHARE:]
    pattern = jnp.concatenate([pattern, flip(pattern, "orient", 4)], axis=0)
    power = add(power, flip(power, "tile", 1))
    power, pattern = lax.optimization_barrier((power, pattern))
    pattern = jnp.concatenate([pattern, flip(pattern, "orient", 1)], axis=0)
    pattern_far = flip(pattern, "orient", 12)
    own = [power] + [flip(power, "orient", mask) for mask in (2, 16, 18)]
    own = jnp.concatenate(own, axis=0)
    other = flip(own, "orient", 1)

    scratch = [
        pltpu.VMEM((8, 2 * TPL, LEN), BF16),
        pltpu.VMEM((8, HALF, 2 * LEN), BF16),
        pltpu.VMEM((4, LEN, 256), BF16),
    ]
    gains, sums = pl.pallas_call(
        search_kernel,
        out_shape=(shaped(F32, 3, HALF, LEN), shaped(F32, 3, VALID, 128)),
        in_specs=[VMEM] * 9,
        out_specs=(VMEM,) * 2,
        scratch_shapes=[pltpu.VMEM((4 * SHARE, LEN), F32)] + scratch,
        compiler_params=limits(28),
        cost_estimate=cost(300, 1),
    )(spec, own, other, wave, pattern, first_tpl, second_tpl, inner, outer)
    parts = pl.pallas_call(
        second_search_kernel,
        out_shape=(shaped(BF16, 3 * PACK + 8, 128),) * 4,
        in_specs=[VMEM] * 7,
        out_specs=(VMEM,) * 4,
        scratch_shapes=scratch + [pltpu.VMEM((3, VALID, 128), F32)],
        compiler_params=limits(28),
        cost_estimate=cost(3600, 4),
    )(gains, sums, pattern_far, first_tpl, second_tpl, inner, outer)
    got = [flip(parts[i], "orient", mask) for i, mask in ((1, 2), (2, 16), (3, 18))]
    scored = pl.pallas_call(
        score_kernel, out_shape=shaped(BF16, 2 * PACK, 128), in_specs=[VMEM] * 4, out_specs=VMEM
    )(parts[0], *got)
    strip = jnp.concatenate([scored] + [flip(scored, "orient", mask) for mask in (4, 8, 12)], axis=0)
    strips = [strip] + [flip(strip, "orient", mask) for mask in (2, 16, 18)]
    twins = [flip(s, "orient", 1) for s in strips]

    def rows_of(step, place):
        return (step ^ place[0], 0, 0)

    return pl.pallas_call(
        spread_kernel,
        out_shape=(shaped(F32, 2, VALID, VALID),) * 2,
        grid_spec=pltpu.PrefetchScalarGridSpec(
            num_scalar_prefetch=1,
            grid=(2,),
            in_specs=[VMEM] * 8,
            out_specs=(pl.BlockSpec((1, VALID, VALID), rows_of),) * 2,
        ),
        compiler_params=limits(16),
    )(at_core().astype(jnp.int32).reshape(1), *strips, *twins)


def solution(mesh):
    placed = (
        P("tile", None, None),
        P("tile", None),
        P("tile", "orient", None, None),
        P("orient", None),
    )
    return jax.shard_map(
        body,
        mesh=mesh,
        in_specs=placed,
        out_specs=(P("tile", None, None), P("tile", None, None)),
        check_vma=False,
    )
```

```python
import math

import jax
import jax.numpy as jnp
import ml_dtypes
import numpy as np
from jax import lax
from jax.experimental import pallas as pl
from jax.experimental.pallas import tpu as pltpu
from jax.sharding import PartitionSpec as P

LEN = 512
TPL = 128
VALID = 384
TILES = 16
SEARCH = 64
HALF = 272
SHARE = 80
PART = 96
PACK = 72
AMPLITUDE = 0.07
DEFOCUS_BASE = 100.0
DEFOCUS_TILT = 0.002
FLOOR_SHARE = 0.25

F32 = jnp.float32
BF16 = jnp.bfloat16


def tables():
    counter = np.arange(LEN)
    angle = 2.0 * np.pi * (counter[:, None] * counter[None, :] % LEN) / LEN
    cos = np.cos(angle).astype(ml_dtypes.bfloat16).astype(np.float32)
    sin = np.sin(angle).astype(ml_dtypes.bfloat16).astype(np.float32)
    both = np.concatenate([cos, sin], 1)
    first_tpl = np.concatenate([cos[:TPL], -sin[:TPL]], 1)
    cos_tpl, sin_tpl = cos[:HALF, :TPL], sin[:HALF, :TPL]
    second_tpl = np.block([[cos_tpl, sin_tpl], [-sin_tpl, cos_tpl]])
    inner = np.zeros((4, 2 * LEN, 256), np.float32)
    for part in range(4):
        cols = slice(PART * part, PART * (part + 1))
        inner[part, :LEN, :PART] = cos[:, cols]
        inner[part, :LEN, 128 : 128 + PART] = sin[:, cols]
        inner[part, LEN:, :PART] = -sin[:, cols]
        inner[part, LEN:, 128 : 128 + PART] = cos[:, cols]
    middle = LEN // 2
    outer = np.concatenate([2.0 * cos[:VALID, :middle], -2.0 * sin[:VALID, :middle]], 1)
    outer[:, 0] = cos[:VALID, 0]
    outer[:, middle] = cos[:VALID, middle]
    tables = (both, first_tpl, second_tpl, inner, outer)
    return [np.asarray(a).astype(ml_dtypes.bfloat16) for a in tables]


def dot(left, right):
    return jnp.dot(left, right, preferred_element_type=F32)


def at_core():
    return lax.axis_index("orient") & 1


def at_column():
    orient = lax.axis_index("orient")
    return (orient >> 4) * 2 + ((orient >> 1) & 1)


def at_group():
    return (lax.axis_index("orient") >> 2) & 3


def pick_kernel(ids, library, out, slabs, sems):
    copies = []
    for step in range(2):
        source = library.at[ids[0, step] % 8, 0]
        copies.append(pltpu.make_async_copy(source, slabs.at[step], sems.at[step]))
        copies[step].start()
    for step in range(2):
        copies[step].wait()
        held = ids[0, step] // 8 == lax.axis_index("tile")
        lanes = slice(TPL * step, TPL * (step + 1))
        out[:, lanes] = jnp.where(held, slabs[step].astype(F32), 0.0).astype(BF16)


def forward_kernel(tile, both, spec, keep, send, stack, power):
    half = dot(tile[at_core()], both[...])
    real, imag = half[:, :LEN].astype(BF16), (-half[:, LEN:]).astype(BF16)
    stack[:LEN, :LEN], stack[LEN:, :LEN] = real, imag
    stack[:LEN, LEN:], stack[LEN:, LEN:] = imag, -real
    result = dot(both[:HALF, :], stack[...])
    spec[...] = result
    power[:HALF] = result[:, :LEN] * result[:, :LEN] + result[:, LEN:] * result[:, LEN:]
    power[HALF:] = jnp.zeros((4 * SHARE - HALF, LEN), F32)
    share = power[pl.ds(pl.multiple_of(at_column() * SHARE, SHARE), SHARE), :]
    left, right = share[:, :256], share[:, 256:]
    low = at_core() == 0
    keep[...] = jnp.where(low, left, right).astype(BF16)
    send[...] = jnp.where(low, right, left).astype(BF16)


def wave_kernel(offsets, out):
    core = at_core()
    shift = (offsets[core, 0] - offsets[core, 1]).astype(F32)
    defocus = DEFOCUS_BASE + DEFOCUS_TILT * shift
    row = lax.broadcasted_iota(jnp.int32, (HALF, 1), 0).astype(F32) * (1.0 / LEN)
    col = lax.broadcasted_iota(jnp.int32, (1, LEN), 1)
    col = jnp.where(col < LEN // 2, col, col - LEN).astype(F32) * (1.0 / LEN)
    row_phase, col_phase = math.pi * defocus * (row * row), math.pi * defocus * (col * col)
    sine, cosine = jnp.sin(col_phase), jnp.cos(col_phase)
    strong = math.sqrt(1.0 - AMPLITUDE * AMPLITUDE)
    by_sine, by_cosine = strong * cosine - AMPLITUDE * sine, strong * sine + AMPLITUDE * cosine
    wave = jnp.sin(row_phase) * by_sine + jnp.cos(row_phase) * by_cosine
    out[...] = jnp.where(row + jnp.abs(col) > 0.0, -wave, 0.0)


def fold(block):
    lane = lax.broadcasted_iota(jnp.int32, (PACK, 128), 1)
    tail = block[PACK:PART]
    moved = [pltpu.roll(tail, 96 - 32 * i, 1) for i in range(3)]
    return jnp.where(lane < PART, block[:PACK], jnp.concatenate(moved, axis=0))


def unfold(block):
    lane = lax.broadcasted_iota(jnp.int32, (24, 128), 1)
    pieces = [pltpu.roll(block[24 * i : 24 * (i + 1)], (32 * i + 32) % 128, 1) for i in range(3)]
    tail = jnp.where(lane < 32, pieces[0], jnp.where(lane < 64, pieces[1], pieces[2]))
    return jnp.concatenate([block, tail], axis=0)


def fold_part(sums, place, tail):
    rows = pl.ds(pl.multiple_of(place * PART, PART), PART)
    folded = [fold(source[rows, :]) for source in sums] + [jnp.zeros((tail, 128), F32)]
    return jnp.concatenate(folded, axis=0).astype(BF16)


def add_maps(pair, rows, middle, scale0, scale1, sums):
    maps = dot(rows, middle)
    map0, map1 = maps[:, :128] * scale0, maps[:, 128:] * scale1
    most, both, power = jnp.maximum(map0, map1), map0 + map1, map0 * map0 + map1 * map1
    peak, total, squares = sums
    peak[...] = most if pair == 0 else jnp.maximum(peak[...], most)
    total[...] = both if pair == 0 else total[...] + both
    squares[...] = power if pair == 0 else squares[...] + power


def base_kernel(own, first, second_tpl, bases, pats, lines):
    pick_patterns(own, pats)
    fill_lines(pats, first, lines)
    for which in range(8):
        bases[which] = dot(second_tpl[...], lines[which]).astype(BF16)


def pick_patterns(source, pats):
    for share in range(4):
        rows = slice((SHARE + TPL) * share + SHARE, (SHARE + TPL) * (share + 1))
        pats[2 * TPL * share : 2 * TPL * share + TPL] = source[rows, :TPL]
        pats[2 * TPL * share + TPL : 2 * TPL * (share + 1)] = source[rows, TPL:]


def fill_lines(pats, first, lines):
    half = dot(pats[...], first[...]).astype(BF16)
    for which in range(8):
        rows = slice(TPL * which, TPL * (which + 1))
        lines[which, :TPL] = half[rows, :LEN]
        lines[which, TPL:] = half[rows, LEN:]


def search_kernel(
    spec, own, other, bases, wave, first, second_tpl, inner, outer, mid, scales, far0, far1,
    gain_r, gain_i, energy_w, power, pats, lines, prod, *sums,
):
    low, group, column = at_core() == 0, at_group(), at_column()
    for share in range(4):
        start = pl.multiple_of((share ^ column) * (SHARE + TPL), 16)
        mine, theirs = [ref[pl.ds(start, SHARE), :].astype(F32) for ref in (own, other)]
        rows = slice(SHARE * share, SHARE * (share + 1))
        power[rows, :256] = jnp.where(low, mine, theirs)
        power[rows, 256:] = jnp.where(low, theirs, mine)
    density = power[:HALF] * (1.0 / TILES)
    row = lax.broadcasted_iota(jnp.int32, (HALF, LEN), 0)
    edge = (row == 0) | (row == LEN // 2)
    count = jnp.where(row > LEN // 2, 0.0, jnp.where(edge, 1.0, 2.0))
    mean = jnp.sum(density * count) * (1.0 / (LEN * LEN))
    gain = wave[...] / jnp.maximum(density, FLOOR_SHARE * mean)
    gain_r[...] = spec[:, :LEN] * gain
    gain_i[...] = spec[:, LEN:] * gain
    energy_w[...] = wave[...] * gain * count * (1.0 / (LEN * LEN))
    top_row = lax.broadcasted_iota(jnp.int32, (LEN // 2, 128), 0) == 0

    pick_patterns(other, pats)
    fill_lines(pats, first, lines)
    rows_far = outer[pl.ds(pl.multiple_of(((group >> 1) ^ 1) * 2 * PART, 2 * PART), 2 * PART), :]
    for which in range(16):
        if which < 8:
            base = bases[which].astype(F32)
        else:
            base = dot(second_tpl[...], lines[which - 8])
        base_r, base_i = base[:HALF], base[HALF:]
        energy = jnp.sum((base_r * base_r + base_i * base_i) * energy_w[...])
        scale = lax.rsqrt(jnp.full((1, 128), energy + 1e-06)) * (1.0 / LEN)
        scales[which : which + 1, :] = scale
        prod[which, :, :LEN] = (gain_r[...] * base_r + gain_i[...] * base_i).astype(BF16)
        prod[which, :, LEN:] = (gain_i[...] * base_r - gain_r[...] * base_i).astype(BF16)
        part = dot(prod[which], inner[...])
        pair, lanes = which // 2, slice(128 * (which % 2), 128 * (which % 2 + 1))
        mid_r, mid_i = part[: LEN // 2, :128], part[: LEN // 2, 128:]
        nyquist = part[LEN // 2 : LEN // 2 + 1, :128]
        mid[pair, : LEN // 2, lanes] = mid_r.astype(BF16)
        mid[pair, LEN // 2 :, lanes] = jnp.where(top_row, nyquist, mid_i).astype(BF16)
        if which % 2 == 1:
            add_maps(pair, rows_far, mid[pair], last, scale, sums)
        last = scale

    far0[...] = fold_part(sums, group & 1, 24)
    far1[...] = fold_part(sums, (group & 1) ^ 1, 24)


def near_kernel(mid, scales, outer, own, near, *sums):
    group = at_group()
    rows = outer[pl.ds(pl.multiple_of((group >> 1) * 2 * PART, 2 * PART), 2 * PART), :]
    for pair in range(8):
        scale0, scale1 = [scales[2 * pair + i : 2 * pair + i + 1, :] for i in range(2)]
        add_maps(pair, rows, mid[pair], scale0, scale1, sums)
    own[...] = fold_part(sums, group & 1, 8)
    near[...] = fold_part(sums, (group & 1) ^ 1, 8)


def score_kernel(own, got1, got2, got3, out):
    blocks = [ref[...].astype(F32) for ref in (own, got1, got2, got3)]
    peak = blocks[0][:PACK]
    for block in blocks[1:]:
        peak = jnp.maximum(peak, block[:PACK])
    total, squares = [
        sum(block[PACK * i : PACK * (i + 1)] for block in blocks) * (1.0 / SEARCH) for i in (1, 2)
    ]
    variance = squares - total * total
    score = (peak - total) * lax.rsqrt(variance + 1e-06)
    block = jnp.concatenate([peak, score], axis=0).astype(BF16)
    out[...] = block


def spread_kernel(place, *refs):
    peak_out, score_out, held = refs[8:]
    lane = lax.broadcasted_iota(jnp.int32, (PART, 128), 1)
    column, group = at_column(), at_group()

    def spread(strips):
        for number, strip in enumerate(strips):
            held[number] = strip[...]
        for index in range(4):
            block = slice(2 * PACK * index, 2 * PACK * (index + 1))
            pieces = [held[column ^ target, block, :].astype(F32) for target in range(4)]
            rows = pl.ds(pl.multiple_of((group ^ index) * PART, PART), PART)
            for slot, out in enumerate((peak_out, score_out)):
                p0, p1, p2, p3 = [unfold(p[PACK * slot : PACK * (slot + 1)]) for p in pieces]
                p1, p2, p3 = [pltpu.roll(p, by, 1) for p, by in ((p1, 96), (p2, 64), (p3, 32))]
                out[0, rows, :128] = jnp.where(lane < 96, p0, p1)
                out[0, rows, 128:256] = jnp.where(lane < 64, p1, p2)
                out[0, rows, 256:] = jnp.where(lane < 32, p2, p3)

    pl.when(pl.program_id(0) == 0)(lambda: spread(refs[:4]))
    pl.when(pl.program_id(0) == 1)(lambda: spread(refs[4:8]))


VMEM = pl.BlockSpec(memory_space=pltpu.VMEM)
SMEM = pl.BlockSpec(memory_space=pltpu.SMEM)


def shaped(dtype, *shape):
    return jax.ShapeDtypeStruct(shape, dtype)


def limits(megabytes):
    return pltpu.CompilerParams(vmem_limit_bytes=megabytes * 1024 * 1024)


def cost(mega_products, megabytes):
    return pl.CostEstimate(
        flops=2_000_000 * mega_products, bytes_accessed=1_000_000 * megabytes, transcendentals=0
    )


def flip(value, axis, mask):
    size = lax.axis_size(axis)
    return lax.ppermute(value, axis, [(i, i ^ mask) for i in range(size)])


def body(micrograph_tiles, tile_offsets, library, orient_ids):
    both, first_tpl, second_tpl, inner, outer = [jnp.asarray(a) for a in tables()]

    pattern = pl.pallas_call(
        pick_kernel,
        out_shape=shaped(BF16, TPL, 2 * TPL),
        in_specs=[SMEM, pl.BlockSpec(memory_space=pl.ANY)],
        out_specs=VMEM,
        scratch_shapes=[pltpu.VMEM((2, TPL, TPL), BF16), pltpu.SemaphoreType.DMA((2,))],
    )(orient_ids, library)
    micrograph_tiles, pattern = lax.optimization_barrier((micrograph_tiles, pattern))
    passed = flip(pattern, "tile", 1)

    spec, power, send = pl.pallas_call(
        forward_kernel,
        out_shape=(shaped(F32, HALF, 2 * LEN), shaped(BF16, SHARE, 256), shaped(BF16, SHARE, 256)),
        in_specs=[VMEM] * 2,
        out_specs=(VMEM,) * 3,
        scratch_shapes=[pltpu.VMEM((2 * LEN, 2 * LEN), BF16), pltpu.VMEM((4 * SHARE, LEN), F32)],
        compiler_params=limits(24),
        cost_estimate=cost(545, 3),
    )(micrograph_tiles, both)
    def add(left, right):
        return (left.astype(F32) + right.astype(F32)).astype(BF16)

    send, passed = lax.optimization_barrier((send, passed))
    message = jnp.concatenate([add(power, flip(send, "orient", 1)), add(pattern, passed)], axis=0)
    message, tile_offsets = lax.optimization_barrier((message, tile_offsets))
    message_2 = flip(message, "tile", 2)
    wave = pl.pallas_call(
        wave_kernel,
        out_shape=shaped(F32, HALF, LEN),
        in_specs=[SMEM],
        out_specs=VMEM,
        cost_estimate=cost(400, 1),
    )(tile_offsets)

    message = add(message, message_2)
    message, wave, inner = lax.optimization_barrier((message, wave, inner))
    message_6 = flip(message, "tile", 6)
    inner = lax.dynamic_index_in_dim(inner, at_column(), 0, keepdims=False)
    message = add(message, message_6)
    message, inner = lax.optimization_barrier((message, inner))
    power, pattern = message[:SHARE], message[SHARE:]
    power = add(power, flip(power, "tile", 1))
    message = jnp.concatenate([power, pattern], axis=0)
    own = [message] + [flip(message, "orient", mask) for mask in (2, 16, 18)]
    own = jnp.concatenate(own, axis=0)
    other = flip(own, "orient", 1)

    sums = [pltpu.VMEM((2 * PART, 128), F32)] * 3
    halves = [pltpu.VMEM((8 * TPL, TPL), BF16), pltpu.VMEM((8, 2 * TPL, LEN), BF16)]
    bases = pl.pallas_call(
        base_kernel,
        out_shape=shaped(BF16, 8, 2 * HALF, LEN),
        in_specs=[VMEM] * 3,
        out_specs=VMEM,
        scratch_shapes=halves,
        compiler_params=limits(24),
        cost_estimate=cost(4000, 4),
    )(own, first_tpl, second_tpl)
    mid, scales, far0, far1 = pl.pallas_call(
        search_kernel,
        out_shape=(shaped(BF16, 8, LEN, 256), shaped(F32, 16, 128))
        + (shaped(BF16, 3 * PACK + 24, 128),) * 2,
        in_specs=[VMEM] * 9,
        out_specs=(VMEM,) * 4,
        scratch_shapes=[
            pltpu.VMEM((HALF, LEN), F32),
            pltpu.VMEM((HALF, LEN), F32),
            pltpu.VMEM((HALF, LEN), F32),
            pltpu.VMEM((4 * SHARE, LEN), F32),
        ]
        + halves
        + [pltpu.VMEM((16, HALF, 2 * LEN), BF16)]
        + sums,
        compiler_params=limits(40),
        cost_estimate=cost(3600, 4),
    )(spec, own, other, bases, wave, first_tpl, second_tpl, inner, outer)
    far = [flip(far0, "orient", 8), flip(far1, "orient", 12)]
    own, near = pl.pallas_call(
        near_kernel,
        out_shape=(shaped(BF16, 3 * PACK + 8, 128),) * 2,
        in_specs=[VMEM] * 3,
        out_specs=(VMEM,) * 2,
        scratch_shapes=sums,
        compiler_params=limits(24),
        cost_estimate=cost(4000, 4),
    )(mid, scales, outer)
    got = [flip(near, "orient", 4)] + far
    scored = pl.pallas_call(
        score_kernel, out_shape=shaped(BF16, 2 * PACK, 128), in_specs=[VMEM] * 4, out_specs=VMEM
    )(own, *got)
    beside, across = flip(scored, "orient", 4), flip(scored, "orient", 12)
    strip = jnp.concatenate([scored, beside, flip(across, "orient", 4), across], axis=0)
    strips = [strip] + [flip(strip, "orient", mask) for mask in (2, 16, 18)]
    twins = [flip(s, "orient", 1) for s in strips]

    def rows_of(step, place):
        return (step ^ place[0], 0, 0)

    return pl.pallas_call(
        spread_kernel,
        out_shape=(shaped(F32, 2, VALID, VALID),) * 2,
        grid_spec=pltpu.PrefetchScalarGridSpec(
            num_scalar_prefetch=1,
            grid=(2,),
            in_specs=[VMEM] * 8,
            out_specs=(pl.BlockSpec((1, VALID, VALID), rows_of),) * 2,
            scratch_shapes=[pltpu.VMEM((4, 8 * PACK, 128), BF16)],
        ),
        compiler_params=limits(16),
    )(at_core().astype(jnp.int32).reshape(1), *strips, *twins)


def solution(mesh):
    placed = (
        P("tile", None, None),
        P("tile", None),
        P("tile", "orient", None, None),
        P("orient", None),
    )
    return jax.shard_map(
        body,
        mesh=mesh,
        in_specs=placed,
        out_specs=(P("tile", None, None), P("tile", None, None)),
        check_vma=False,
    )
```

```python
import math

import jax
import jax.numpy as jnp
import ml_dtypes
import numpy as np
from jax import lax
from jax.experimental import pallas as pl
from jax.experimental.pallas import tpu as pltpu
from jax.sharding import PartitionSpec as P

LEN = 512
TPL = 128
VALID = 384
TILES = 16
SEARCH = 64
HALF = 272
SHARE = 80
PART = 96
PACK = 72
AMPLITUDE = 0.07
DEFOCUS_BASE = 100.0
DEFOCUS_TILT = 0.002
FLOOR_SHARE = 0.25

F32 = jnp.float32
BF16 = jnp.bfloat16


def tables():
    counter = np.arange(LEN)
    angle = 2.0 * np.pi * (counter[:, None] * counter[None, :] % LEN) / LEN
    cos = np.cos(angle).astype(ml_dtypes.bfloat16).astype(np.float32)
    sin = np.sin(angle).astype(ml_dtypes.bfloat16).astype(np.float32)
    both = np.concatenate([cos, sin], 1)
    first_tpl = np.concatenate([cos[:TPL], -sin[:TPL]], 1)
    cos_tpl, sin_tpl = cos[:HALF, :TPL], sin[:HALF, :TPL]
    second_tpl = np.block([[cos_tpl, sin_tpl], [-sin_tpl, cos_tpl]])
    inner = np.zeros((4, 2 * LEN, 256), np.float32)
    for part in range(4):
        cols = slice(PART * part, PART * (part + 1))
        inner[part, :LEN, :PART] = cos[:, cols]
        inner[part, :LEN, 128 : 128 + PART] = sin[:, cols]
        inner[part, LEN:, :PART] = -sin[:, cols]
        inner[part, LEN:, 128 : 128 + PART] = cos[:, cols]
    middle = LEN // 2
    outer = np.concatenate([2.0 * cos[:VALID, :middle], -2.0 * sin[:VALID, :middle]], 1)
    outer[:, 0] = cos[:VALID, 0]
    outer[:, middle] = cos[:VALID, middle]
    tables = (both, first_tpl, second_tpl, inner, outer)
    return [np.asarray(a).astype(ml_dtypes.bfloat16) for a in tables]


def dot(left, right):
    return jnp.dot(left, right, preferred_element_type=F32)


def at_core():
    return lax.axis_index("orient") & 1


def at_column():
    orient = lax.axis_index("orient")
    return (orient >> 4) * 2 + ((orient >> 1) & 1)


def at_group():
    return (lax.axis_index("orient") >> 2) & 3


def pick_kernel(ids, library, out, slabs, sems):
    copies = []
    for step in range(2):
        source = library.at[ids[0, step] % 8, 0]
        copies.append(pltpu.make_async_copy(source, slabs.at[step], sems.at[step]))
        copies[step].start()
    for step in range(2):
        copies[step].wait()
        held = ids[0, step] // 8 == lax.axis_index("tile")
        lanes = slice(TPL * step, TPL * (step + 1))
        out[:, lanes] = jnp.where(held, slabs[step].astype(F32), 0.0).astype(BF16)


def forward_kernel(tile, both, spec, keep, send, stack, power):
    half = dot(tile[at_core()], both[...])
    real, imag = half[:, :LEN].astype(BF16), (-half[:, LEN:]).astype(BF16)
    stack[:LEN, :LEN], stack[LEN:, :LEN] = real, imag
    stack[:LEN, LEN:], stack[LEN:, LEN:] = imag, -real
    result = dot(both[:HALF, :], stack[...])
    spec[...] = result
    power[:HALF] = result[:, :LEN] * result[:, :LEN] + result[:, LEN:] * result[:, LEN:]
    power[HALF:] = jnp.zeros((4 * SHARE - HALF, LEN), F32)
    share = power[pl.ds(pl.multiple_of(at_column() * SHARE, SHARE), SHARE), :]
    left, right = share[:, :256], share[:, 256:]
    low = at_core() == 0
    keep[...] = jnp.where(low, left, right).astype(BF16)
    send[...] = jnp.where(low, right, left).astype(BF16)


def wave_kernel(offsets, out):
    core = at_core()
    shift = (offsets[core, 0] - offsets[core, 1]).astype(F32)
    defocus = DEFOCUS_BASE + DEFOCUS_TILT * shift
    row = lax.broadcasted_iota(jnp.int32, (HALF, 1), 0).astype(F32) * (1.0 / LEN)
    col = lax.broadcasted_iota(jnp.int32, (1, LEN), 1)
    col = jnp.where(col < LEN // 2, col, col - LEN).astype(F32) * (1.0 / LEN)
    row_phase, col_phase = math.pi * defocus * (row * row), math.pi * defocus * (col * col)
    sine, cosine = jnp.sin(col_phase), jnp.cos(col_phase)
    strong = math.sqrt(1.0 - AMPLITUDE * AMPLITUDE)
    by_sine, by_cosine = strong * cosine - AMPLITUDE * sine, strong * sine + AMPLITUDE * cosine
    wave = jnp.sin(row_phase) * by_sine + jnp.cos(row_phase) * by_cosine
    out[...] = jnp.where(row + jnp.abs(col) > 0.0, -wave, 0.0)


def fold(block):
    lane = lax.broadcasted_iota(jnp.int32, (PACK, 128), 1)
    tail = block[PACK:PART]
    moved = [pltpu.roll(tail, 96 - 32 * i, 1) for i in range(3)]
    return jnp.where(lane < PART, block[:PACK], jnp.concatenate(moved, axis=0))


def unfold(block):
    lane = lax.broadcasted_iota(jnp.int32, (24, 128), 1)
    pieces = [pltpu.roll(block[24 * i : 24 * (i + 1)], (32 * i + 32) % 128, 1) for i in range(3)]
    tail = jnp.where(lane < 32, pieces[0], jnp.where(lane < 64, pieces[1], pieces[2]))
    return jnp.concatenate([block, tail], axis=0)


def fold_part(sums, place, tail):
    rows = pl.ds(pl.multiple_of(place * PART, PART), PART)
    folded = [fold(source[rows, :]) for source in sums] + [jnp.zeros((tail, 128), F32)]
    return jnp.concatenate(folded, axis=0).astype(BF16)


def add_maps(pair, rows, middle, scale0, scale1, sums):
    maps = dot(rows, middle)
    map0, map1 = maps[:, :128] * scale0, maps[:, 128:] * scale1
    most, both, power = jnp.maximum(map0, map1), map0 + map1, map0 * map0 + map1 * map1
    peak, total, squares = sums
    peak[...] = most if pair == 0 else jnp.maximum(peak[...], most)
    total[...] = both if pair == 0 else total[...] + both
    squares[...] = power if pair == 0 else squares[...] + power


def base_kernel(own, first, second_tpl, bases, pats, lines):
    pick_patterns(own, pats)
    fill_lines(pats, first, lines)
    for which in range(8):
        bases[which] = dot(second_tpl[...], lines[which]).astype(BF16)


def pick_patterns(source, pats):
    for share in range(4):
        rows = slice((SHARE + TPL) * share + SHARE, (SHARE + TPL) * (share + 1))
        pats[2 * TPL * share : 2 * TPL * share + TPL] = source[rows, :TPL]
        pats[2 * TPL * share + TPL : 2 * TPL * (share + 1)] = source[rows, TPL:]


def fill_lines(pats, first, lines):
    half = dot(pats[...], first[...]).astype(BF16)
    for which in range(8):
        rows = slice(TPL * which, TPL * (which + 1))
        lines[which, :TPL] = half[rows, :LEN]
        lines[which, TPL:] = half[rows, LEN:]


def search_kernel(
    spec, own, other, bases, wave, first, second_tpl, inner, outer, mid, scales, far0, far1,
    gain_r, gain_i, energy_w, power, pats, lines, prod, *sums,
):
    low, group, column = at_core() == 0, at_group(), at_column()
    for share in range(4):
        start = pl.multiple_of((share ^ column) * (SHARE + TPL), 16)
        mine, theirs = [ref[pl.ds(start, SHARE), :].astype(F32) for ref in (own, other)]
        rows = slice(SHARE * share, SHARE * (share + 1))
        power[rows, :256] = jnp.where(low, mine, theirs)
        power[rows, 256:] = jnp.where(low, theirs, mine)
    density = power[:HALF] * (1.0 / TILES)
    row = lax.broadcasted_iota(jnp.int32, (HALF, LEN), 0)
    edge = (row == 0) | (row == LEN // 2)
    count = jnp.where(row > LEN // 2, 0.0, jnp.where(edge, 1.0, 2.0))
    mean = jnp.sum(density * count) * (1.0 / (LEN * LEN))
    gain = wave[...] / jnp.maximum(density, FLOOR_SHARE * mean)
    gain_r[...] = (spec[:, :LEN] * gain).astype(BF16)
    gain_i[...] = (spec[:, LEN:] * gain).astype(BF16)
    energy_w[...] = wave[...] * gain * count * (1.0 / (LEN * LEN))
    top_row = lax.broadcasted_iota(jnp.int32, (LEN // 2, 128), 0) == 0

    pick_patterns(other, pats)
    fill_lines(pats, first, lines)
    rows_far = outer[pl.ds(pl.multiple_of(((group >> 1) ^ 1) * 2 * PART, 2 * PART), 2 * PART), :]
    for which in range(16):
        base = bases[which] if which < 8 else dot(second_tpl[...], lines[which - 8])
        rounded, base = base.astype(BF16), base.astype(F32)
        base_r, base_i = base[:HALF], base[HALF:]
        energy = jnp.sum((base_r * base_r + base_i * base_i) * energy_w[...])
        scale = lax.rsqrt(jnp.full((1, 128), energy + 1e-06)) * (1.0 / LEN)
        scales[which : which + 1, :] = scale
        flat_r, flat_i = rounded[:HALF], rounded[HALF:]
        prod[which, :, :LEN] = gain_r[...] * flat_r + gain_i[...] * flat_i
        prod[which, :, LEN:] = gain_i[...] * flat_r - gain_r[...] * flat_i
        part = dot(prod[which], inner[...])
        pair, lanes = which // 2, slice(128 * (which % 2), 128 * (which % 2 + 1))
        mid_r, mid_i = part[: LEN // 2, :128], part[: LEN // 2, 128:]
        nyquist = part[LEN // 2 : LEN // 2 + 1, :128]
        mid[pair, : LEN // 2, lanes] = mid_r.astype(BF16)
        mid[pair, LEN // 2 :, lanes] = jnp.where(top_row, nyquist, mid_i).astype(BF16)
        if which % 2 == 1:
            add_maps(pair, rows_far, mid[pair], last, scale, sums)
        last = scale

    far0[...] = fold_part(sums, group & 1, 24)
    far1[...] = fold_part(sums, (group & 1) ^ 1, 24)


def near_kernel(mid, scales, outer, own, near, *sums):
    group = at_group()
    rows = outer[pl.ds(pl.multiple_of((group >> 1) * 2 * PART, 2 * PART), 2 * PART), :]
    for pair in range(8):
        scale0, scale1 = [scales[2 * pair + i : 2 * pair + i + 1, :] for i in range(2)]
        add_maps(pair, rows, mid[pair], scale0, scale1, sums)
    own[...] = fold_part(sums, group & 1, 8)
    near[...] = fold_part(sums, (group & 1) ^ 1, 8)


def score_kernel(own, got1, got2, got3, out):
    blocks = [ref[...].astype(F32) for ref in (own, got1, got2, got3)]
    peak = blocks[0][:PACK]
    for block in blocks[1:]:
        peak = jnp.maximum(peak, block[:PACK])
    total, squares = [
        sum(block[PACK * i : PACK * (i + 1)] for block in blocks) * (1.0 / SEARCH) for i in (1, 2)
    ]
    variance = squares - total * total
    score = (peak - total) * lax.rsqrt(variance + 1e-06)
    block = jnp.concatenate([peak, score], axis=0).astype(BF16)
    out[...] = block


def spread_kernel(place, *refs):
    strips, (peak_out, score_out, held) = refs[:4], refs[-3:]
    lane = lax.broadcasted_iota(jnp.int32, (PART, 128), 1)
    column, group = at_column(), at_group()
    for number, strip in enumerate(strips):
        held[number] = strip[...]
    for index in range(4):
        block = slice(2 * PACK * index, 2 * PACK * (index + 1))
        pieces = [held[column ^ target, block, :].astype(F32) for target in range(4)]
        rows = pl.ds(pl.multiple_of((group ^ index) * PART, PART), PART)
        for slot, out in enumerate((peak_out, score_out)):
            p0, p1, p2, p3 = [unfold(p[PACK * slot : PACK * (slot + 1)]) for p in pieces]
            p1, p2, p3 = [pltpu.roll(p, by, 1) for p, by in ((p1, 96), (p2, 64), (p3, 32))]
            out[0, rows, :128] = jnp.where(lane < 96, p0, p1)
            out[0, rows, 128:256] = jnp.where(lane < 64, p1, p2)
            out[0, rows, 256:] = jnp.where(lane < 32, p2, p3)


def spread(tile, strips, filled):
    return pl.pallas_call(
        spread_kernel,
        out_shape=(shaped(F32, 2, VALID, VALID),) * 2,
        grid_spec=pltpu.PrefetchScalarGridSpec(
            num_scalar_prefetch=1,
            grid=(1,),
            in_specs=[VMEM] * 4 + [pl.BlockSpec(memory_space=pl.ANY)] * len(filled),
            out_specs=(pl.BlockSpec((1, VALID, VALID), lambda i, tile: (tile[0], 0, 0)),) * 2,
            scratch_shapes=[pltpu.VMEM((4, 8 * PACK, 128), BF16)],
        ),
        input_output_aliases={5 + i: i for i in range(len(filled))},
        compiler_params=limits(16),
        cost_estimate=cost(1000, 2),
    )(tile.astype(jnp.int32).reshape(1), *strips, *filled)


VMEM = pl.BlockSpec(memory_space=pltpu.VMEM)
SMEM = pl.BlockSpec(memory_space=pltpu.SMEM)


def shaped(dtype, *shape):
    return jax.ShapeDtypeStruct(shape, dtype)


def limits(megabytes):
    return pltpu.CompilerParams(vmem_limit_bytes=megabytes * 1024 * 1024)


def cost(mega_products, megabytes):
    return pl.CostEstimate(
        flops=2_000_000 * mega_products, bytes_accessed=1_000_000 * megabytes, transcendentals=0
    )


def flip(value, axis, mask):
    size = lax.axis_size(axis)
    return lax.ppermute(value, axis, [(i, i ^ mask) for i in range(size)])


def body(micrograph_tiles, tile_offsets, library, orient_ids):
    both, first_tpl, second_tpl, inner, outer = [jnp.asarray(a) for a in tables()]

    pattern = pl.pallas_call(
        pick_kernel,
        out_shape=shaped(BF16, TPL, 2 * TPL),
        in_specs=[SMEM, pl.BlockSpec(memory_space=pl.ANY)],
        out_specs=VMEM,
        scratch_shapes=[pltpu.VMEM((2, TPL, TPL), BF16), pltpu.SemaphoreType.DMA((2,))],
    )(orient_ids, library)
    micrograph_tiles, pattern = lax.optimization_barrier((micrograph_tiles, pattern))
    passed = flip(pattern, "tile", 1)

    spec, power, send = pl.pallas_call(
        forward_kernel,
        out_shape=(shaped(F32, HALF, 2 * LEN), shaped(BF16, SHARE, 256), shaped(BF16, SHARE, 256)),
        in_specs=[VMEM] * 2,
        out_specs=(VMEM,) * 3,
        scratch_shapes=[pltpu.VMEM((2 * LEN, 2 * LEN), BF16), pltpu.VMEM((4 * SHARE, LEN), F32)],
        compiler_params=limits(24),
        cost_estimate=cost(545, 3),
    )(micrograph_tiles, both)
    def add(left, right):
        return (left.astype(F32) + right.astype(F32)).astype(BF16)

    send, passed = lax.optimization_barrier((send, passed))
    message = jnp.concatenate([add(power, flip(send, "orient", 1)), add(pattern, passed)], axis=0)
    message, tile_offsets = lax.optimization_barrier((message, tile_offsets))
    message_2 = flip(message, "tile", 2)
    wave = pl.pallas_call(
        wave_kernel,
        out_shape=shaped(F32, HALF, LEN),
        in_specs=[SMEM],
        out_specs=VMEM,
        cost_estimate=cost(400, 1),
    )(tile_offsets)

    message = add(message, message_2)
    message, wave, inner = lax.optimization_barrier((message, wave, inner))
    message_6 = flip(message, "tile", 6)
    inner = lax.dynamic_index_in_dim(inner, at_column(), 0, keepdims=False)
    message = add(message, message_6)
    message, inner = lax.optimization_barrier((message, inner))
    power, pattern = message[:SHARE], message[SHARE:]
    power = add(power, flip(power, "tile", 1))
    message = jnp.concatenate([power, pattern], axis=0)
    own = [message] + [flip(message, "orient", mask) for mask in (2, 16, 18)]
    own = jnp.concatenate(own, axis=0)
    other = flip(own, "orient", 1)

    sums = [pltpu.VMEM((2 * PART, 128), F32)] * 3
    halves = [pltpu.VMEM((8 * TPL, TPL), BF16), pltpu.VMEM((8, 2 * TPL, LEN), BF16)]
    bases = pl.pallas_call(
        base_kernel,
        out_shape=shaped(BF16, 8, 2 * HALF, LEN),
        in_specs=[VMEM] * 3,
        out_specs=VMEM,
        scratch_shapes=halves,
        compiler_params=limits(24),
        cost_estimate=cost(4000, 4),
    )(own, first_tpl, second_tpl)
    mid, scales, far0, far1 = pl.pallas_call(
        search_kernel,
        out_shape=(shaped(BF16, 8, LEN, 256), shaped(F32, 16, 128))
        + (shaped(BF16, 3 * PACK + 24, 128),) * 2,
        in_specs=[VMEM] * 9,
        out_specs=(VMEM,) * 4,
        scratch_shapes=[
            pltpu.VMEM((HALF, LEN), BF16),
            pltpu.VMEM((HALF, LEN), BF16),
            pltpu.VMEM((HALF, LEN), F32),
            pltpu.VMEM((4 * SHARE, LEN), F32),
        ]
        + halves
        + [pltpu.VMEM((16, HALF, 2 * LEN), BF16)]
        + sums,
        compiler_params=limits(40),
        cost_estimate=cost(3600, 4),
    )(spec, own, other, bases, wave, first_tpl, second_tpl, inner, outer)
    far = [flip(far0, "orient", 8), flip(far1, "orient", 12)]
    own, near = pl.pallas_call(
        near_kernel,
        out_shape=(shaped(BF16, 3 * PACK + 8, 128),) * 2,
        in_specs=[VMEM] * 3,
        out_specs=(VMEM,) * 2,
        scratch_shapes=sums,
        compiler_params=limits(24),
        cost_estimate=cost(4000, 4),
    )(mid, scales, outer)
    got = [flip(near, "orient", 4)] + far
    scored = pl.pallas_call(
        score_kernel, out_shape=shaped(BF16, 2 * PACK, 128), in_specs=[VMEM] * 4, out_specs=VMEM
    )(own, *got)
    beside, across = flip(scored, "orient", 4), flip(scored, "orient", 12)
    strip = jnp.concatenate([scored, beside, flip(across, "orient", 4), across], axis=0)
    strips = [strip] + [flip(strip, "orient", mask) for mask in (2, 16, 18)]
    twins = [flip(s, "orient", 1) for s in strips]

    return spread(1 - at_core(), twins, spread(at_core(), strips, ()))


def solution(mesh):
    placed = (
        P("tile", None, None),
        P("tile", None),
        P("tile", "orient", None, None),
        P("orient", None),
    )
    return jax.shard_map(
        body,
        mesh=mesh,
        in_specs=placed,
        out_specs=(P("tile", None, None), P("tile", None, None)),
        check_vma=False,
    )
```

```python
import math

import jax
import jax.numpy as jnp
import ml_dtypes
import numpy as np
from jax import lax
from jax.experimental import pallas as pl
from jax.experimental.pallas import tpu as pltpu
from jax.sharding import PartitionSpec as P

LEN = 512
TPL = 128
VALID = 384
TILES = 16
SEARCH = 64
HALF = 272
SHARE = 80
PART = 96
PACK = 72
AMPLITUDE = 0.07
DEFOCUS_BASE = 100.0
DEFOCUS_TILT = 0.002
FLOOR_SHARE = 0.25

F32 = jnp.float32
BF16 = jnp.bfloat16


def tables():
    counter = np.arange(LEN)
    angle = 2.0 * np.pi * (counter[:, None] * counter[None, :] % LEN) / LEN
    cos = np.cos(angle).astype(ml_dtypes.bfloat16).astype(np.float32)
    sin = np.sin(angle).astype(ml_dtypes.bfloat16).astype(np.float32)
    both = np.stack([np.concatenate([t[:, at : at + 256] for t in (cos, sin)], 1) for at in (0, 256)])
    first_tpl = np.concatenate([cos[:TPL], -sin[:TPL]], 1)
    cos_tpl, sin_tpl = cos[:HALF, :TPL], sin[:HALF, :TPL]
    second_tpl = np.block([[cos_tpl, sin_tpl], [-sin_tpl, cos_tpl]])
    inner = np.zeros((4, 2 * LEN, 256), np.float32)
    for part in range(4):
        cols = slice(PART * part, PART * (part + 1))
        inner[part, :LEN, :PART] = cos[:, cols]
        inner[part, :LEN, 128 : 128 + PART] = sin[:, cols]
        inner[part, LEN:, :PART] = -sin[:, cols]
        inner[part, LEN:, 128 : 128 + PART] = cos[:, cols]
    middle = LEN // 2
    outer = np.concatenate([2.0 * cos[:VALID, :middle], -2.0 * sin[:VALID, :middle]], 1)
    outer[:, 0] = cos[:VALID, 0]
    outer[:, middle] = cos[:VALID, middle]
    tables = (both, first_tpl, second_tpl, inner, outer)
    return [np.asarray(a).astype(ml_dtypes.bfloat16) for a in tables]


def dot(left, right):
    return jnp.dot(left, right, preferred_element_type=F32)


def at_core():
    return lax.axis_index("orient") & 1


def at_column():
    orient = lax.axis_index("orient")
    return (orient >> 4) * 2 + ((orient >> 1) & 1)


def at_group():
    return (lax.axis_index("orient") >> 2) & 3


def pick_kernel(ids, library, out, slabs, sems):
    copies = []
    for step in range(2):
        source = library.at[ids[0, step] % 8, 0]
        copies.append(pltpu.make_async_copy(source, slabs.at[step], sems.at[step]))
        copies[step].start()
    for step in range(2):
        copies[step].wait()
        held = ids[0, step] // 8 == lax.axis_index("tile")
        lanes = slice(TPL * step, TPL * (step + 1))
        out[:, lanes] = jnp.where(held, slabs[step].astype(F32), 0.0).astype(BF16)


def forward_kernel(tiles, both, keep, send, share, stack, power):
    core = at_core()
    specs = []
    for tile in range(2):
        half = dot(tiles[tile], both[core])
        real, imag = half[:, :256].astype(BF16), (-half[:, 256:]).astype(BF16)
        for part in range(2):
            rows, at = slice(256 * part, 256 * (part + 1)), LEN * part
            stack[tile, at : at + 256, :256] = real[rows]
            stack[tile, at : at + 256, 256:] = imag[rows]
            stack[tile, at + 256 : at + LEN, :256] = imag[rows]
            stack[tile, at + 256 : at + LEN, 256:] = -real[rows]
        spec = dot(both[0, :HALF, :], stack[tile, :LEN]) + dot(both[1, :HALF, :], stack[tile, LEN:])
        specs.append(spec)
    keep[...] = jnp.where(core == 0, specs[0], specs[1])
    send[...] = jnp.where(core == 0, specs[1], specs[0])
    squares = [spec * spec for spec in specs]
    squares = squares[0] + squares[1]
    power[:HALF] = squares[:, :256] + squares[:, 256:]
    power[HALF:] = jnp.zeros((4 * SHARE - HALF, 256), F32)
    start = pl.multiple_of(at_column() * SHARE, SHARE)
    share[...] = power[pl.ds(start, SHARE), :].astype(BF16)


def wave_kernel(offsets, out):
    core = at_core()
    shift = (offsets[core, 0] - offsets[core, 1]).astype(F32)
    defocus = DEFOCUS_BASE + DEFOCUS_TILT * shift
    row = lax.broadcasted_iota(jnp.int32, (HALF, 1), 0).astype(F32) * (1.0 / LEN)
    col = lax.broadcasted_iota(jnp.int32, (1, LEN), 1)
    col = jnp.where(col < LEN // 2, col, col - LEN).astype(F32) * (1.0 / LEN)
    row_phase, col_phase = math.pi * defocus * (row * row), math.pi * defocus * (col * col)
    sine, cosine = jnp.sin(col_phase), jnp.cos(col_phase)
    strong = math.sqrt(1.0 - AMPLITUDE * AMPLITUDE)
    by_sine, by_cosine = strong * cosine - AMPLITUDE * sine, strong * sine + AMPLITUDE * cosine
    wave = jnp.sin(row_phase) * by_sine + jnp.cos(row_phase) * by_cosine
    out[...] = jnp.where(row + jnp.abs(col) > 0.0, -wave, 0.0)


def fold(block):
    lane = lax.broadcasted_iota(jnp.int32, (PACK, 128), 1)
    tail = block[PACK:PART]
    moved = [pltpu.roll(tail, 96 - 32 * i, 1) for i in range(3)]
    return jnp.where(lane < PART, block[:PACK], jnp.concatenate(moved, axis=0))


def unfold(block):
    lane = lax.broadcasted_iota(jnp.int32, (24, 128), 1)
    pieces = [pltpu.roll(block[24 * i : 24 * (i + 1)], (32 * i + 32) % 128, 1) for i in range(3)]
    tail = jnp.where(lane < 32, pieces[0], jnp.where(lane < 64, pieces[1], pieces[2]))
    return jnp.concatenate([block, tail], axis=0)


def fold_part(sums, place, tail):
    rows = pl.ds(pl.multiple_of(place * PART, PART), PART)
    folded = [fold(source[rows, :]) for source in sums] + [jnp.zeros((tail, 128), F32)]
    return jnp.concatenate(folded, axis=0).astype(BF16)


def add_maps(pair, rows, middle, scale0, scale1, sums):
    maps = dot(rows, middle)
    map0, map1 = maps[:, :128] * scale0, maps[:, 128:] * scale1
    most, both, power = jnp.maximum(map0, map1), map0 + map1, map0 * map0 + map1 * map1
    peak, total, squares = sums
    peak[...] = most if pair == 0 else jnp.maximum(peak[...], most)
    total[...] = both if pair == 0 else total[...] + both
    squares[...] = power if pair == 0 else squares[...] + power


def base_kernel(own, first, second_tpl, bases, pats, lines):
    pick_patterns(own, pats)
    fill_lines(pats, first, lines)
    for which in range(8):
        bases[which] = dot(second_tpl[...], lines[which]).astype(BF16)


def pick_patterns(source, pats):
    for share in range(4):
        rows = slice((SHARE + TPL) * share + SHARE, (SHARE + TPL) * (share + 1))
        pats[2 * TPL * share : 2 * TPL * share + TPL] = source[rows, :TPL]
        pats[2 * TPL * share + TPL : 2 * TPL * (share + 1)] = source[rows, TPL:]


def fill_lines(pats, first, lines):
    half = dot(pats[...], first[...]).astype(BF16)
    for which in range(8):
        rows = slice(TPL * which, TPL * (which + 1))
        lines[which, :TPL] = half[rows, :LEN]
        lines[which, TPL:] = half[rows, LEN:]


def search_kernel(
    spec, spec_other, own, other, bases, wave, first, second_tpl, inner, outer, mid, scales, far0, far1,
    gain_r, gain_i, energy_w, power, pats, lines, prod, *sums,
):
    low, group, column = at_core() == 0, at_group(), at_column()
    for share in range(4):
        start = pl.multiple_of((share ^ column) * (SHARE + TPL), 16)
        mine, theirs = [ref[pl.ds(start, SHARE), :].astype(F32) for ref in (own, other)]
        rows = slice(SHARE * share, SHARE * (share + 1))
        power[rows, :256] = jnp.where(low, mine, theirs)
        power[rows, 256:] = jnp.where(low, theirs, mine)
    density = power[:HALF] * (1.0 / TILES)
    row = lax.broadcasted_iota(jnp.int32, (HALF, LEN), 0)
    edge = (row == 0) | (row == LEN // 2)
    count = jnp.where(row > LEN // 2, 0.0, jnp.where(edge, 1.0, 2.0))
    mean = jnp.sum(density * count) * (1.0 / (LEN * LEN))
    gain = wave[...] / jnp.maximum(density, FLOOR_SHARE * mean)
    mine, theirs = spec[...], spec_other[...]
    left, right = jnp.where(low, mine, theirs), jnp.where(low, theirs, mine)
    for part, source in enumerate((left, right)):
        lanes = slice(256 * part, 256 * (part + 1))
        gain_r[:, lanes] = (source[:, :256] * gain[:, lanes]).astype(BF16)
        gain_i[:, lanes] = (source[:, 256:] * gain[:, lanes]).astype(BF16)
    energy_w[...] = wave[...] * gain * count * (1.0 / (LEN * LEN))
    top_row = lax.broadcasted_iota(jnp.int32, (LEN // 2, 128), 0) == 0

    pick_patterns(other, pats)
    fill_lines(pats, first, lines)
    rows_far = outer[pl.ds(pl.multiple_of(((group >> 1) ^ 1) * 2 * PART, 2 * PART), 2 * PART), :]
    for which in range(16):
        base = bases[which] if which < 8 else dot(second_tpl[...], lines[which - 8])
        rounded, base = base.astype(BF16), base.astype(F32)
        base_r, base_i = base[:HALF], base[HALF:]
        energy = jnp.sum((base_r * base_r + base_i * base_i) * energy_w[...])
        scale = lax.rsqrt(jnp.full((1, 128), energy + 1e-06)) * (1.0 / LEN)
        scales[which : which + 1, :] = scale
        flat_r, flat_i = rounded[:HALF], rounded[HALF:]
        prod[which, :, :LEN] = gain_r[...] * flat_r + gain_i[...] * flat_i
        prod[which, :, LEN:] = gain_i[...] * flat_r - gain_r[...] * flat_i
        part = dot(prod[which], inner[...])
        pair, lanes = which // 2, slice(128 * (which % 2), 128 * (which % 2 + 1))
        mid_r, mid_i = part[: LEN // 2, :128], part[: LEN // 2, 128:]
        nyquist = part[LEN // 2 : LEN // 2 + 1, :128]
        mid[pair, : LEN // 2, lanes] = mid_r.astype(BF16)
        mid[pair, LEN // 2 :, lanes] = jnp.where(top_row, nyquist, mid_i).astype(BF16)
        if which % 2 == 1:
            add_maps(pair, rows_far, mid[pair], last, scale, sums)
        last = scale

    far0[...] = fold_part(sums, group & 1, 24)
    far1[...] = fold_part(sums, (group & 1) ^ 1, 24)


def near_kernel(mid, scales, outer, own, near, *sums):
    group = at_group()
    rows = outer[pl.ds(pl.multiple_of((group >> 1) * 2 * PART, 2 * PART), 2 * PART), :]
    for pair in range(8):
        scale0, scale1 = [scales[2 * pair + i : 2 * pair + i + 1, :] for i in range(2)]
        add_maps(pair, rows, mid[pair], scale0, scale1, sums)
    own[...] = fold_part(sums, group & 1, 8)
    near[...] = fold_part(sums, (group & 1) ^ 1, 8)


def score_kernel(own, got1, got2, got3, out):
    blocks = [ref[...].astype(F32) for ref in (own, got1, got2, got3)]
    peak = blocks[0][:PACK]
    for block in blocks[1:]:
        peak = jnp.maximum(peak, block[:PACK])
    total, squares = [
        sum(block[PACK * i : PACK * (i + 1)] for block in blocks) * (1.0 / SEARCH) for i in (1, 2)
    ]
    variance = squares - total * total
    score = (peak - total) * lax.rsqrt(variance + 1e-06)
    block = jnp.concatenate([peak, score], axis=0).astype(BF16)
    out[...] = block


def spread_kernel(place, *refs):
    strips, (peak_out, score_out, held) = refs[:4], refs[-3:]
    lane = lax.broadcasted_iota(jnp.int32, (PART, 128), 1)
    column, group = at_column(), at_group()
    for number, strip in enumerate(strips):
        held[number] = strip[...]
    for index in range(4):
        block = slice(2 * PACK * index, 2 * PACK * (index + 1))
        pieces = [held[column ^ target, block, :].astype(F32) for target in range(4)]
        rows = pl.ds(pl.multiple_of((group ^ index) * PART, PART), PART)
        for slot, out in enumerate((peak_out, score_out)):
            p0, p1, p2, p3 = [unfold(p[PACK * slot : PACK * (slot + 1)]) for p in pieces]
            p1, p2, p3 = [pltpu.roll(p, by, 1) for p, by in ((p1, 96), (p2, 64), (p3, 32))]
            out[0, rows, :128] = jnp.where(lane < 96, p0, p1)
            out[0, rows, 128:256] = jnp.where(lane < 64, p1, p2)
            out[0, rows, 256:] = jnp.where(lane < 32, p2, p3)


def spread(tile, strips, filled):
    return pl.pallas_call(
        spread_kernel,
        out_shape=(shaped(F32, 2, VALID, VALID),) * 2,
        grid_spec=pltpu.PrefetchScalarGridSpec(
            num_scalar_prefetch=1,
            grid=(1,),
            in_specs=[VMEM] * 4 + [pl.BlockSpec(memory_space=pl.ANY)] * len(filled),
            out_specs=(pl.BlockSpec((1, VALID, VALID), lambda i, tile: (tile[0], 0, 0)),) * 2,
            scratch_shapes=[pltpu.VMEM((4, 8 * PACK, 128), BF16)],
        ),
        input_output_aliases={5 + i: i for i in range(len(filled))},
        compiler_params=limits(16),
        cost_estimate=cost(1000, 2),
    )(tile.astype(jnp.int32).reshape(1), *strips, *filled)


VMEM = pl.BlockSpec(memory_space=pltpu.VMEM)
SMEM = pl.BlockSpec(memory_space=pltpu.SMEM)


def shaped(dtype, *shape):
    return jax.ShapeDtypeStruct(shape, dtype)


def limits(megabytes):
    return pltpu.CompilerParams(vmem_limit_bytes=megabytes * 1024 * 1024)


def cost(mega_products, megabytes):
    return pl.CostEstimate(
        flops=2_000_000 * mega_products, bytes_accessed=1_000_000 * megabytes, transcendentals=0
    )


def flip(value, axis, mask):
    size = lax.axis_size(axis)
    return lax.ppermute(value, axis, [(i, i ^ mask) for i in range(size)])


def body(micrograph_tiles, tile_offsets, library, orient_ids):
    both, first_tpl, second_tpl, inner, outer = [jnp.asarray(a) for a in tables()]

    pattern = pl.pallas_call(
        pick_kernel,
        out_shape=shaped(BF16, TPL, 2 * TPL),
        in_specs=[SMEM, pl.BlockSpec(memory_space=pl.ANY)],
        out_specs=VMEM,
        scratch_shapes=[pltpu.VMEM((2, TPL, TPL), BF16), pltpu.SemaphoreType.DMA((2,))],
    )(orient_ids, library)
    micrograph_tiles, pattern = lax.optimization_barrier((micrograph_tiles, pattern))
    passed = flip(pattern, "tile", 1)

    spec, send, power = pl.pallas_call(
        forward_kernel,
        out_shape=(shaped(F32, HALF, LEN), shaped(F32, HALF, LEN), shaped(BF16, SHARE, 256)),
        in_specs=[VMEM] * 2,
        out_specs=(VMEM,) * 3,
        scratch_shapes=[pltpu.VMEM((2, 2 * LEN, LEN), BF16), pltpu.VMEM((4 * SHARE, 256), F32)],
        compiler_params=limits(24),
        cost_estimate=cost(545, 3),
    )(micrograph_tiles, both)

    def add(left, right):
        return (left.astype(F32) + right.astype(F32)).astype(BF16)

    power, passed = lax.optimization_barrier((power, passed))
    message = jnp.concatenate([power, add(pattern, passed)], axis=0)
    message, tile_offsets = lax.optimization_barrier((message, tile_offsets))
    message_2 = flip(message, "tile", 2)
    spec_other = flip(send, "orient", 1)
    wave = pl.pallas_call(
        wave_kernel,
        out_shape=shaped(F32, HALF, LEN),
        in_specs=[SMEM],
        out_specs=VMEM,
        cost_estimate=cost(400, 1),
    )(tile_offsets)

    message = add(message, message_2)
    message, wave, inner = lax.optimization_barrier((message, wave, inner))
    message_6 = flip(message, "tile", 6)
    inner = lax.dynamic_index_in_dim(inner, at_column(), 0, keepdims=False)
    message = add(message, message_6)
    message, inner = lax.optimization_barrier((message, inner))
    power, pattern = message[:SHARE], message[SHARE:]
    power = add(power, flip(power, "tile", 1))
    message = jnp.concatenate([power, pattern], axis=0)
    own = [message] + [flip(message, "orient", mask) for mask in (2, 16, 18)]
    own = jnp.concatenate(own, axis=0)
    other = flip(own, "orient", 1)

    sums = [pltpu.VMEM((2 * PART, 128), F32)] * 3
    halves = [pltpu.VMEM((8 * TPL, TPL), BF16), pltpu.VMEM((8, 2 * TPL, LEN), BF16)]
    bases = pl.pallas_call(
        base_kernel,
        out_shape=shaped(BF16, 8, 2 * HALF, LEN),
        in_specs=[VMEM] * 3,
        out_specs=VMEM,
        scratch_shapes=halves,
        compiler_params=limits(24),
        cost_estimate=cost(4000, 4),
    )(own, first_tpl, second_tpl)
    mid, scales, far0, far1 = pl.pallas_call(
        search_kernel,
        out_shape=(shaped(BF16, 8, LEN, 256), shaped(F32, 16, 128))
        + (shaped(BF16, 3 * PACK + 24, 128),) * 2,
        in_specs=[VMEM] * 10,
        out_specs=(VMEM,) * 4,
        scratch_shapes=[
            pltpu.VMEM((HALF, LEN), BF16),
            pltpu.VMEM((HALF, LEN), BF16),
            pltpu.VMEM((HALF, LEN), F32),
            pltpu.VMEM((4 * SHARE, LEN), F32),
        ]
        + halves
        + [pltpu.VMEM((16, HALF, 2 * LEN), BF16)]
        + sums,
        compiler_params=limits(40),
        cost_estimate=cost(3600, 4),
    )(spec, spec_other, own, other, bases, wave, first_tpl, second_tpl, inner, outer)
    far = [flip(far0, "orient", 8), flip(far1, "orient", 12)]
    own, near = pl.pallas_call(
        near_kernel,
        out_shape=(shaped(BF16, 3 * PACK + 8, 128),) * 2,
        in_specs=[VMEM] * 3,
        out_specs=(VMEM,) * 2,
        scratch_shapes=sums,
        compiler_params=limits(24),
        cost_estimate=cost(4000, 4),
    )(mid, scales, outer)
    got = [flip(near, "orient", 4)] + far
    scored = pl.pallas_call(
        score_kernel, out_shape=shaped(BF16, 2 * PACK, 128), in_specs=[VMEM] * 4, out_specs=VMEM
    )(own, *got)
    beside, across = flip(scored, "orient", 4), flip(scored, "orient", 12)
    strip = jnp.concatenate([scored, beside, flip(across, "orient", 4), across], axis=0)
    strips = [strip] + [flip(strip, "orient", mask) for mask in (2, 16, 18)]
    twins = [flip(s, "orient", 1) for s in strips]

    return spread(1 - at_core(), twins, spread(at_core(), strips, ()))


def solution(mesh):
    placed = (
        P("tile", None, None),
        P("tile", None),
        P("tile", "orient", None, None),
        P("orient", None),
    )
    return jax.shard_map(
        body,
        mesh=mesh,
        in_specs=placed,
        out_specs=(P("tile", None, None), P("tile", None, None)),
        check_vma=False,
    )
```

```python
import math

import jax
import jax.numpy as jnp
import ml_dtypes
import numpy as np
from jax import lax
from jax.experimental import pallas as pl
from jax.experimental.pallas import tpu as pltpu
from jax.sharding import PartitionSpec as P

LEN = 512
TPL = 128
VALID = 384
TILES = 16
SEARCH = 64
HALF = 272
SHARE = 80
PART = 96
PACK = 72
AMPLITUDE = 0.07
DEFOCUS_BASE = 100.0
DEFOCUS_TILT = 0.002
FLOOR_SHARE = 0.25

F32 = jnp.float32
BF16 = jnp.bfloat16


def tables():
    counter = np.arange(LEN)
    angle = 2.0 * np.pi * (counter[:, None] * counter[None, :] % LEN) / LEN
    cos = np.cos(angle).astype(ml_dtypes.bfloat16).astype(np.float32)
    sin = np.sin(angle).astype(ml_dtypes.bfloat16).astype(np.float32)
    both = np.stack([np.concatenate([t[:, at : at + 256] for t in (cos, sin)], 1) for at in (0, 256)])
    first_tpl = np.concatenate([cos[:TPL], -sin[:TPL]], 1)
    cos_tpl, sin_tpl = cos[:HALF, :TPL], sin[:HALF, :TPL]
    second_tpl = np.block([[cos_tpl, sin_tpl], [-sin_tpl, cos_tpl]])
    inner = np.zeros((4, 2 * LEN, 256), np.float32)
    for part in range(4):
        cols = slice(PART * part, PART * (part + 1))
        inner[part, :LEN, :PART] = cos[:, cols]
        inner[part, :LEN, 128 : 128 + PART] = sin[:, cols]
        inner[part, LEN:, :PART] = -sin[:, cols]
        inner[part, LEN:, 128 : 128 + PART] = cos[:, cols]
    middle = LEN // 2
    outer = np.concatenate([2.0 * cos[:VALID, :middle], -2.0 * sin[:VALID, :middle]], 1)
    outer[:, 0] = cos[:VALID, 0]
    outer[:, middle] = cos[:VALID, middle]
    tables = (both, first_tpl, second_tpl, inner, outer)
    return [np.asarray(a).astype(ml_dtypes.bfloat16) for a in tables]


def dot(left, right):
    return jnp.dot(left, right, preferred_element_type=F32)


def at_core():
    return lax.axis_index("orient") & 1


def at_column():
    orient = lax.axis_index("orient")
    return (orient >> 4) * 2 + ((orient >> 1) & 1)


def at_group():
    return (lax.axis_index("orient") >> 2) & 3


def pick_kernel(ids, library, out, slabs, sems):
    copies = []
    for step in range(2):
        source = library.at[ids[0, step] % 8, 0]
        copies.append(pltpu.make_async_copy(source, slabs.at[step], sems.at[step]))
        copies[step].start()
    for step in range(2):
        copies[step].wait()
        held = ids[0, step] // 8 == lax.axis_index("tile")
        lanes = slice(TPL * step, TPL * (step + 1))
        out[:, lanes] = jnp.where(held, slabs[step].astype(F32), 0.0).astype(BF16)


def forward_kernel(tiles, both, keep, send, share, stack, power):
    core = at_core()
    specs = []
    for tile in range(2):
        half = dot(tiles[tile], both[core])
        real, imag = half[:, :256].astype(BF16), (-half[:, 256:]).astype(BF16)
        for part in range(2):
            rows, at = slice(256 * part, 256 * (part + 1)), LEN * part
            stack[tile, at : at + 256, :256] = real[rows]
            stack[tile, at : at + 256, 256:] = imag[rows]
            stack[tile, at + 256 : at + LEN, :256] = imag[rows]
            stack[tile, at + 256 : at + LEN, 256:] = -real[rows]
        spec = dot(both[0, :HALF, :], stack[tile, :LEN]) + dot(both[1, :HALF, :], stack[tile, LEN:])
        specs.append(spec)
    keep[...] = jnp.where(core == 0, specs[0], specs[1])
    send[...] = jnp.where(core == 0, specs[1], specs[0])
    squares = [spec * spec for spec in specs]
    squares = squares[0] + squares[1]
    power[:HALF] = squares[:, :256] + squares[:, 256:]
    power[HALF:] = jnp.zeros((4 * SHARE - HALF, 256), F32)
    start = pl.multiple_of(at_column() * SHARE, SHARE)
    share[...] = power[pl.ds(start, SHARE), :].astype(BF16)


def wave_kernel(offsets, out):
    core = at_core()
    shift = (offsets[core, 0] - offsets[core, 1]).astype(F32)
    defocus = DEFOCUS_BASE + DEFOCUS_TILT * shift
    row = lax.broadcasted_iota(jnp.int32, (HALF, 1), 0).astype(F32) * (1.0 / LEN)
    col = lax.broadcasted_iota(jnp.int32, (1, LEN), 1)
    col = jnp.where(col < LEN // 2, col, col - LEN).astype(F32) * (1.0 / LEN)
    row_phase, col_phase = math.pi * defocus * (row * row), math.pi * defocus * (col * col)
    sine, cosine = jnp.sin(col_phase), jnp.cos(col_phase)
    strong = math.sqrt(1.0 - AMPLITUDE * AMPLITUDE)
    by_sine, by_cosine = strong * cosine - AMPLITUDE * sine, strong * sine + AMPLITUDE * cosine
    wave = jnp.sin(row_phase) * by_sine + jnp.cos(row_phase) * by_cosine
    out[...] = jnp.where(row + jnp.abs(col) > 0.0, -wave, 0.0)


def fold(block):
    lane = lax.broadcasted_iota(jnp.int32, (PACK, 128), 1)
    tail = block[PACK:PART]
    moved = [pltpu.roll(tail, 96 - 32 * i, 1) for i in range(3)]
    return jnp.where(lane < PART, block[:PACK], jnp.concatenate(moved, axis=0))


def unfold(block):
    lane = lax.broadcasted_iota(jnp.int32, (24, 128), 1)
    pieces = [pltpu.roll(block[24 * i : 24 * (i + 1)], (32 * i + 32) % 128, 1) for i in range(3)]
    tail = jnp.where(lane < 32, pieces[0], jnp.where(lane < 64, pieces[1], pieces[2]))
    return jnp.concatenate([block, tail], axis=0)


def fold_part(sums, place, tail):
    rows = pl.ds(pl.multiple_of(place * PART, PART), PART)
    folded = [fold(source[rows, :]) for source in sums] + [jnp.zeros((tail, 128), F32)]
    return jnp.concatenate(folded, axis=0).astype(BF16)


def add_maps(pair, rows, middle, scale0, scale1, sums):
    maps = dot(rows, middle)
    map0, map1 = maps[:, :128] * scale0, maps[:, 128:] * scale1
    most, both, power = jnp.maximum(map0, map1), map0 + map1, map0 * map0 + map1 * map1
    peak, total, squares = sums
    peak[...] = most if pair == 0 else jnp.maximum(peak[...], most)
    total[...] = both if pair == 0 else total[...] + both
    squares[...] = power if pair == 0 else squares[...] + power


def base_kernel(own, first, second_tpl, bases, pats, lines):
    pick_patterns(own, pats)
    fill_lines(pats, first, lines)
    for which in range(8):
        bases[which] = dot(second_tpl[...], lines[which]).astype(BF16)


def pick_patterns(source, pats):
    for share in range(4):
        rows = slice((SHARE + TPL) * share + SHARE, (SHARE + TPL) * (share + 1))
        pats[2 * TPL * share : 2 * TPL * share + TPL] = source[rows, :TPL]
        pats[2 * TPL * share + TPL : 2 * TPL * (share + 1)] = source[rows, TPL:]


def fill_lines(pats, first, lines):
    half = dot(pats[...], first[...]).astype(BF16)
    for which in range(8):
        rows = slice(TPL * which, TPL * (which + 1))
        lines[which, :TPL] = half[rows, :LEN]
        lines[which, TPL:] = half[rows, LEN:]


def search_kernel(
    spec, spec_other, own, other, bases, wave, first, second_tpl, inner, outer, mid, scales, far0, far1,
    gain_r, gain_i, energy_w, power, pats, lines, prod, *sums,
):
    low, group, column = at_core() == 0, at_group(), at_column()
    for share in range(4):
        start = pl.multiple_of((share ^ column) * (SHARE + TPL), 16)
        mine, theirs = [ref[pl.ds(start, SHARE), :].astype(F32) for ref in (own, other)]
        rows = slice(SHARE * share, SHARE * (share + 1))
        power[rows, :256] = jnp.where(low, mine, theirs)
        power[rows, 256:] = jnp.where(low, theirs, mine)
    density = power[:HALF] * (1.0 / TILES)
    row = lax.broadcasted_iota(jnp.int32, (HALF, LEN), 0)
    edge = (row == 0) | (row == LEN // 2)
    count = jnp.where(row > LEN // 2, 0.0, jnp.where(edge, 1.0, 2.0))
    mean = jnp.sum(density * count) * (1.0 / (LEN * LEN))
    gain = wave[...] / jnp.maximum(density, FLOOR_SHARE * mean)
    mine, theirs = spec[...], spec_other[...]
    left, right = jnp.where(low, mine, theirs), jnp.where(low, theirs, mine)
    for part, source in enumerate((left, right)):
        lanes = slice(256 * part, 256 * (part + 1))
        gain_r[:, lanes] = (source[:, :256] * gain[:, lanes]).astype(BF16)
        gain_i[:, lanes] = (source[:, 256:] * gain[:, lanes]).astype(BF16)
    energy_w[...] = wave[...] * gain * count * (1.0 / (LEN * LEN))
    top_row = lax.broadcasted_iota(jnp.int32, (LEN // 2, 128), 0) == 0

    pick_patterns(other, pats)
    fill_lines(pats, first, lines)
    rows_far = outer[pl.ds(pl.multiple_of(((group >> 1) ^ 1) * 2 * PART, 2 * PART), 2 * PART), :]
    for which in range(16):
        base = bases[which] if which < 8 else dot(second_tpl[...], lines[which - 8])
        rounded, base = base.astype(BF16), base.astype(F32)
        base_r, base_i = base[:HALF], base[HALF:]
        energy = jnp.sum((base_r * base_r + base_i * base_i) * energy_w[...])
        scale = lax.rsqrt(jnp.full((1, 128), energy + 1e-06)) * (1.0 / LEN)
        scales[which : which + 1, :] = scale
        flat_r, flat_i = rounded[:HALF], rounded[HALF:]
        prod[which, :, :LEN] = gain_r[...] * flat_r + gain_i[...] * flat_i
        prod[which, :, LEN:] = gain_i[...] * flat_r - gain_r[...] * flat_i
        part = dot(prod[which], inner[...])
        pair, lanes = which // 2, slice(128 * (which % 2), 128 * (which % 2 + 1))
        mid_r, mid_i = part[: LEN // 2, :128], part[: LEN // 2, 128:]
        nyquist = part[LEN // 2 : LEN // 2 + 1, :128]
        mid[pair, : LEN // 2, lanes] = mid_r.astype(BF16)
        mid[pair, LEN // 2 :, lanes] = jnp.where(top_row, nyquist, mid_i).astype(BF16)
        if which % 2 == 1:
            add_maps(pair, rows_far, mid[pair], last, scale, sums)
        last = scale

    far0[...] = fold_part(sums, group & 1, 24)
    far1[...] = fold_part(sums, (group & 1) ^ 1, 24)


def near_kernel(mid, scales, outer, own, near, *sums):
    group = at_group()
    rows = outer[pl.ds(pl.multiple_of((group >> 1) * 2 * PART, 2 * PART), 2 * PART), :]
    for pair in range(8):
        scale0, scale1 = [scales[2 * pair + i : 2 * pair + i + 1, :] for i in range(2)]
        add_maps(pair, rows, mid[pair], scale0, scale1, sums)
    own[...] = fold_part(sums, group & 1, 8)
    near[...] = fold_part(sums, (group & 1) ^ 1, 8)


def score_kernel(own, got1, got2, got3, out):
    blocks = [ref[...].astype(F32) for ref in (own, got1, got2, got3)]
    peak = blocks[0][:PACK]
    for block in blocks[1:]:
        peak = jnp.maximum(peak, block[:PACK])
    total, squares = [
        sum(block[PACK * i : PACK * (i + 1)] for block in blocks) * (1.0 / SEARCH) for i in (1, 2)
    ]
    variance = squares - total * total
    score = (peak - total) * lax.rsqrt(variance + 1e-06)
    block = jnp.concatenate([peak, score], axis=0).astype(BF16)
    out[...] = block


def spread_kernel(place, *refs):
    strips, (peak_out, score_out, held) = refs[:4], refs[-3:]
    lane = lax.broadcasted_iota(jnp.int32, (PART, 128), 1)
    column, group = at_column(), at_group()
    for number, strip in enumerate(strips):
        held[number] = strip[...]
    for index in range(4):
        block = slice(2 * PACK * index, 2 * PACK * (index + 1))
        pieces = [held[column ^ target, block, :].astype(F32) for target in range(4)]
        rows = pl.ds(pl.multiple_of((group ^ index) * PART, PART), PART)
        for slot, out in enumerate((peak_out, score_out)):
            p0, p1, p2, p3 = [unfold(p[PACK * slot : PACK * (slot + 1)]) for p in pieces]
            p1, p2, p3 = [pltpu.roll(p, by, 1) for p, by in ((p1, 96), (p2, 64), (p3, 32))]
            out[0, rows, :128] = jnp.where(lane < 96, p0, p1)
            out[0, rows, 128:256] = jnp.where(lane < 64, p1, p2)
            out[0, rows, 256:] = jnp.where(lane < 32, p2, p3)


def spread(tile, strips, filled):
    return pl.pallas_call(
        spread_kernel,
        out_shape=(shaped(F32, 2, VALID, VALID),) * 2,
        grid_spec=pltpu.PrefetchScalarGridSpec(
            num_scalar_prefetch=1,
            grid=(1,),
            in_specs=[VMEM] * 4 + [pl.BlockSpec(memory_space=pl.ANY)] * len(filled),
            out_specs=(pl.BlockSpec((1, VALID, VALID), lambda i, tile: (tile[0], 0, 0)),) * 2,
            scratch_shapes=[pltpu.VMEM((4, 8 * PACK, 128), BF16)],
        ),
        input_output_aliases={5 + i: i for i in range(len(filled))},
        compiler_params=limits(16),
        cost_estimate=cost(1000, 2),
    )(tile.astype(jnp.int32).reshape(1), *strips, *filled)


VMEM = pl.BlockSpec(memory_space=pltpu.VMEM)
SMEM = pl.BlockSpec(memory_space=pltpu.SMEM)


def shaped(dtype, *shape):
    return jax.ShapeDtypeStruct(shape, dtype)


def limits(megabytes):
    return pltpu.CompilerParams(vmem_limit_bytes=megabytes * 1024 * 1024)


def cost(mega_products, megabytes):
    return pl.CostEstimate(
        flops=2_000_000 * mega_products, bytes_accessed=1_000_000 * megabytes, transcendentals=0
    )


def flip(value, axis, mask):
    size = lax.axis_size(axis)
    return lax.ppermute(value, axis, [(i, i ^ mask) for i in range(size)])


def body(micrograph_tiles, tile_offsets, library, orient_ids):
    both, first_tpl, second_tpl, inner, outer = [jnp.asarray(a) for a in tables()]

    pattern = pl.pallas_call(
        pick_kernel,
        out_shape=shaped(BF16, TPL, 2 * TPL),
        in_specs=[SMEM, pl.BlockSpec(memory_space=pl.ANY)],
        out_specs=VMEM,
        scratch_shapes=[pltpu.VMEM((2, TPL, TPL), BF16), pltpu.SemaphoreType.DMA((2,))],
    )(orient_ids, library)
    micrograph_tiles, pattern = lax.optimization_barrier((micrograph_tiles, pattern))
    passed = flip(pattern, "tile", 1)

    spec, send, power = pl.pallas_call(
        forward_kernel,
        out_shape=(shaped(F32, HALF, LEN), shaped(F32, HALF, LEN), shaped(BF16, SHARE, 256)),
        in_specs=[VMEM] * 2,
        out_specs=(VMEM,) * 3,
        scratch_shapes=[pltpu.VMEM((2, 2 * LEN, LEN), BF16), pltpu.VMEM((4 * SHARE, 256), F32)],
        compiler_params=limits(24),
        cost_estimate=cost(545, 3),
    )(micrograph_tiles, both)

    def add(left, right):
        return (left.astype(F32) + right.astype(F32)).astype(BF16)

    power, passed = lax.optimization_barrier((power, passed))
    message = jnp.concatenate([power, add(pattern, passed)], axis=0)
    message, tile_offsets = lax.optimization_barrier((message, tile_offsets))
    message_2 = flip(message, "tile", 2)
    spec_other = flip(send, "orient", 1)
    wave = pl.pallas_call(
        wave_kernel,
        out_shape=shaped(F32, HALF, LEN),
        in_specs=[SMEM],
        out_specs=VMEM,
        cost_estimate=cost(400, 1),
    )(tile_offsets)

    message = add(message, message_2)
    message, wave, inner, spec_other = lax.optimization_barrier((message, wave, inner, spec_other))
    message_6 = flip(message, "tile", 6)
    inner = lax.dynamic_index_in_dim(inner, at_column(), 0, keepdims=False)
    message = add(message, message_6)
    message, inner = lax.optimization_barrier((message, inner))
    power, pattern = message[:SHARE], message[SHARE:]
    power = add(power, flip(power, "tile", 1))
    message = jnp.concatenate([power, pattern], axis=0)
    own = [message] + [flip(message, "orient", mask) for mask in (2, 16, 18)]
    own = jnp.concatenate(own, axis=0)
    other = flip(own, "orient", 1)

    sums = [pltpu.VMEM((2 * PART, 128), F32)] * 3
    halves = [pltpu.VMEM((8 * TPL, TPL), BF16), pltpu.VMEM((8, 2 * TPL, LEN), BF16)]
    bases = pl.pallas_call(
        base_kernel,
        out_shape=shaped(BF16, 8, 2 * HALF, LEN),
        in_specs=[VMEM] * 3,
        out_specs=VMEM,
        scratch_shapes=halves,
        compiler_params=limits(24),
        cost_estimate=cost(4000, 4),
    )(own, first_tpl, second_tpl)
    mid, scales, far0, far1 = pl.pallas_call(
        search_kernel,
        out_shape=(shaped(BF16, 8, LEN, 256), shaped(F32, 16, 128))
        + (shaped(BF16, 3 * PACK + 24, 128),) * 2,
        in_specs=[VMEM] * 10,
        out_specs=(VMEM,) * 4,
        scratch_shapes=[
            pltpu.VMEM((HALF, LEN), BF16),
            pltpu.VMEM((HALF, LEN), BF16),
            pltpu.VMEM((HALF, LEN), F32),
            pltpu.VMEM((4 * SHARE, LEN), F32),
        ]
        + halves
        + [pltpu.VMEM((16, HALF, 2 * LEN), BF16)]
        + sums,
        compiler_params=limits(40),
        cost_estimate=cost(3600, 4),
    )(spec, spec_other, own, other, bases, wave, first_tpl, second_tpl, inner, outer)
    far = [flip(far0, "orient", 8), flip(far1, "orient", 12)]
    own, near = pl.pallas_call(
        near_kernel,
        out_shape=(shaped(BF16, 3 * PACK + 8, 128),) * 2,
        in_specs=[VMEM] * 3,
        out_specs=(VMEM,) * 2,
        scratch_shapes=sums,
        compiler_params=limits(24),
        cost_estimate=cost(4000, 4),
    )(mid, scales, outer)
    got = [flip(near, "orient", 4)] + far
    scored = pl.pallas_call(
        score_kernel, out_shape=shaped(BF16, 2 * PACK, 128), in_specs=[VMEM] * 4, out_specs=VMEM
    )(own, *got)
    beside, across = flip(scored, "orient", 4), flip(scored, "orient", 12)
    strip = jnp.concatenate([scored, beside, flip(across, "orient", 4), across], axis=0)
    strips = [strip] + [flip(strip, "orient", mask) for mask in (2, 16, 18)]
    twins = [flip(s, "orient", 1) for s in strips]

    return spread(1 - at_core(), twins, spread(at_core(), strips, ()))


def solution(mesh):
    placed = (
        P("tile", None, None),
        P("tile", None),
        P("tile", "orient", None, None),
        P("orient", None),
    )
    return jax.shard_map(
        body,
        mesh=mesh,
        in_specs=placed,
        out_specs=(P("tile", None, None), P("tile", None, None)),
        check_vma=False,
    )
```
